256 devices in a mesh: group: 4 (over z_hi, core), fsdp: 64 (over y, x, z_lo).
Axes of the slice: x: 4, y: 4, z: 8 (z_hi: 2, z_lo: 4; z = z_hi * 4 + z_lo), core: 2. Of those that a mesh axis runs over, the one named last changes fastest.
Arguments:
- hidden_rows: bfloat16 [4, 32768, 4096], P('group', 'fsdp'), may hold values from -16 to 16
- out_grad: bfloat16 [4, 32768, 1024], P('group', 'fsdp'), may hold values from -6 to 6
- params: bfloat16 [4, 4096, 1024], P('group', 'fsdp'), may hold values from -3 to 3
- first_moment: bfloat16 [4, 4096, 1024], P('group', 'fsdp'), may hold values from -1.8 to 1.8
- second_moment: bfloat16 [4, 4096, 1024], P('group', 'fsdp'), may hold values from 0.099609375 to 2
- anchor: bfloat16 [4096, 1024], P('fsdp', 'group'), may hold values from -2 to 2
- outer_momentum: bfloat16 [4096, 1024], P('fsdp', 'group'), may hold values from -4 to 4
Outputs:
- layer_out: bfloat16 [4, 32768, 1024], P('group', 'fsdp')
- input_grad: bfloat16 [4, 32768, 4096], P('group', 'fsdp')
- new_params: bfloat16 [4096, 1024], P('fsdp')
- new_first: bfloat16 [4, 4096, 1024], P('group', 'fsdp')
- new_second: bfloat16 [4, 4096, 1024], P('group', 'fsdp')
- new_momentum: bfloat16 [4096, 1024], P('fsdp', 'group')
The draws below stay inside these ranges and needn't reach their ends.
All inputs are finite; a program needn't handle non-finite values.
Results may differ from the reference program's by a relative error of at most 0.001.
Values may be sent and summed in bfloat16 or wider, within the bound.
A program may use at most 128 MiB of HBM per device.

```python
import math
import jax
import jax.numpy as jnp
from jax import lax

D = 1024
FF = 4096
GROUPS = 4
TOKENS = 32768


def shared_normal(key):
    return jax.random.truncated_normal(key, -4.0, 4.0, (FF, D), jnp.float32)


def draw_anchor(key, part):
    base = shared_normal(key)
    return (0.5 * base).astype(jnp.bfloat16)


def draw_params(key, part):
    base = shared_normal(key)
    key = jax.random.fold_in(key, 11)
    common_key, group_key = jax.random.split(key)
    common = jax.random.truncated_normal(common_key, -4.0, 4.0, (FF, D), jnp.float32)
    spread = jax.random.truncated_normal(group_key, -4.0, 4.0, (GROUPS, FF, D), jnp.float32)
    return (0.5 * base[None] + 0.1 * common[None] + 0.15 * spread).astype(jnp.bfloat16)


def draw_first_moment(key, part):
    key = jax.random.fold_in(key, 23)
    common_key, group_key = jax.random.split(key)
    common = jax.random.truncated_normal(common_key, -4.0, 4.0, (FF, D), jnp.float32)
    spread = jax.random.truncated_normal(group_key, -4.0, 4.0, (GROUPS, FF, D), jnp.float32)
    return (0.3 * common[None] + 0.15 * spread).astype(jnp.bfloat16)


def raised(result, stream_key, source, target, blocks, factor):
    owner, partner = [(jnp.arange(result.shape[position]) // (result.shape[position] // blocks)).reshape([-1 if axis == position else 1 for axis in range(result.ndim)]) for position in (source, target)]
    chosen = jax.random.permutation(stream_key, blocks)[partner]
    strong = (owner == chosen) | (owner == (partner + blocks // 2) % blocks)
    return jnp.where(strong, factor * result, result)


def steps_of(own_key, extent, cuts, least, largest):
    loudness = 1.0
    for dim, blocks in cuts:
        heights = jax.random.uniform(jax.random.fold_in(jax.random.fold_in(own_key, 6), dim), (blocks,), jnp.float32, least / len(cuts), largest / len(cuts))
        loudness = loudness * jnp.repeat(jnp.exp(heights), extent[dim] // blocks).reshape((-1,) + (1,) * (len(extent) - 1 - dim))
    return loudness


def gaussian(rng, dims, scale, limit, shards=(), dtype=jnp.bfloat16):
    level = steps_of(rng, dims, shards, -0.22, 0.18) if shards else 1.0
    drawn = jax.random.normal(rng, dims, jnp.float32) * scale * level
    return jnp.minimum(jnp.maximum(drawn, -limit), limit).astype(dtype)


def heavy_noise(key, dims, deviation, bound, cuts, heavy, held_as=jnp.bfloat16):
    values = deviation * jax.random.normal(key, dims, jnp.float32)
    if cuts:
        values = values * steps_of(key, dims, cuts, -0.22, 0.18)
    return jnp.clip(raised(values, jax.random.fold_in(key, 3), *heavy), -bound, bound).astype(held_as)


def setup_inputs(seed: int = 0) -> dict:
    splits = jax.random.split(jax.random.key(seed), 8)
    return {
        "hidden_rows": heavy_noise(splits[0], (GROUPS, TOKENS, FF), 1.0, 16.0, ((0, 4), (1, 64)), (1, 2, 64, 4.0)),
        "out_grad": gaussian(splits[1], (GROUPS, TOKENS, D), 1.0, 6.0, ((0, 4), (1, 64))),
        "params": draw_params(jax.random.fold_in(splits[7], 71), 0),
        "first_moment": draw_first_moment(jax.random.fold_in(splits[7], 71), 0),
        "second_moment": jnp.clip(jnp.exp(math.log(2.0) - 2.9996462 * jax.random.uniform(splits[4], (GROUPS, FF, D), jnp.float32) ** steps_of(splits[4], (GROUPS, FF, D), ((0, 4), (1, 64)), -0.2, 0.2)), 0.099609375, 2.0).astype(jnp.bfloat16),
        "anchor": draw_anchor(jax.random.fold_in(splits[7], 71), 0),
        "outer_momentum": gaussian(splits[6], (FF, D), 0.25, 4.0, ((0, 64), (1, 4))),
    }


beta_first = 0.9
beta_second = 0.95
adam_eps = 1e-08
learn_rate = 0.1
decay_rate = 0.1
outer_rate = 0.7
outer_beta = 0.9

def reference(hidden_rows, out_grad, params, first_moment, second_moment, anchor, outer_momentum):
    scale_forward = FF ** (-0.5)
    scale_backward = D ** (-0.5)
    scale_gradient = TOKENS ** (-0.5)
    outputs = []
    back_list = []
    first_list = []
    second_list = []
    summed = jnp.zeros((FF, D), jnp.float32)
    for member in range(GROUPS):
        hidden = hidden_rows[member]
        weight = params[member]
        cotangent = out_grad[member]
        forward = jnp.dot(hidden, weight, preferred_element_type=jnp.float32)
        outputs.append((forward * scale_forward).astype(jnp.bfloat16))
        backward = lax.dot_general(cotangent, weight, (((1,), (1,)), ((), ())), preferred_element_type=jnp.float32)
        back_list.append((backward * scale_backward).astype(jnp.bfloat16))
        gradient = lax.dot_general(hidden, cotangent, (((0,), (0,)), ((), ())), preferred_element_type=jnp.float32) * scale_gradient
        first_new = beta_first * first_moment[member].astype(jnp.float32) + (1.0 - beta_first) * gradient
        second_new = beta_second * second_moment[member].astype(jnp.float32) + (1.0 - beta_second) * gradient * gradient
        first_list.append(first_new.astype(jnp.bfloat16))
        second_list.append(second_new.astype(jnp.bfloat16))
        weight_full = weight.astype(jnp.float32)
        inner_params = weight_full - learn_rate * (first_new / (jnp.sqrt(second_new) + adam_eps) + decay_rate * weight_full)
        summed = summed + inner_params
    average = summed / GROUPS
    anchor_full = anchor.astype(jnp.float32)
    pseudo_grad = anchor_full - average
    momentum = outer_beta * outer_momentum.astype(jnp.float32) + pseudo_grad
    updated = anchor_full - outer_rate * (pseudo_grad + outer_beta * momentum)
    return (jnp.stack(outputs), jnp.stack(back_list), updated.astype(jnp.bfloat16), jnp.stack(first_list), jnp.stack(second_list), momentum.astype(jnp.bfloat16))
```

```python
import jax
import jax.numpy as jnp
from jax import lax
from jax.experimental import pallas as pl
from jax.experimental.pallas import tpu as pltpu
from jax.sharding import PartitionSpec as P

D = 1024
FF = 4096
TOKENS = 32768
BLOCK = 64
LOCAL = 512
CHUNKS = 4
ROWS = BLOCK // CHUNKS
HALF = D // 2
QUARTER = D // 4
MIB = 1 << 20

beta_first = 0.9
beta_second = 0.95
adam_eps = 1e-08
learn_rate = 0.1
decay_rate = 0.1
outer_rate = 0.7
outer_beta = 0.9

bf16 = jnp.bfloat16
f32 = jnp.float32


def kernel(
    h_hbm, g_hbm, w_hbm, fm, sm, an, om,
    lo_hbm, ig_hbm, np_out, nf_out, ns_out, nm_out,
    h, g, gr, wf, ht, htr, part, o1, n1, s1, sums, o2, n2, s2, plane, zin, inner, gin, share, lo, ig,
    in_sem, out_sem,
    wz_ss, wz_rs, ag_ss, ag_rs, ex_ss, ex_rs, r1_ss, r1_rs, r2_ss, r2_rs, zz_ss, zz_rs, gi_ss, gi_rs, np_ss, np_rs,
):
    me = lax.axis_index("fsdp")
    grp = lax.axis_index("group")
    z, x, y = lax.rem(me, 4), lax.rem(me // 4, 4), me // 16
    parity, level = lax.rem(z, 2), z // 2

    def at(xx, yy, zz):
        return {"fsdp": (yy * 4 + xx) * 4 + zz}

    def near(axis, step):
        if axis == 0:
            return at(lax.rem(x + step + 4, 4), y, z)
        return at(x, lax.rem(y + step + 4, 4), z)

    def peer(e):
        core, high = lax.rem(grp, 2), grp // 2
        core = 1 - core if e & 1 else core
        high = 1 - high if e & 2 else high
        return high * 2 + core

    def copy(src, dst, ss, rs, device):
        return pltpu.make_async_remote_copy(
            src_ref=src, dst_ref=dst, send_sem=ss, recv_sem=rs, device_id=device, device_id_type=pl.DeviceIdType.MESH
        )

    zpair = at(x, y, z + 1 - 2 * parity)
    zcross = at(x, y, lax.rem(z + 2, 4))
    steps = (1, -1)

    load_g = pltpu.make_async_copy(g_hbm, g, in_sem.at[0])
    load_h = pltpu.make_async_copy(h_hbm, h, in_sem.at[1])
    load_w = pltpu.make_async_copy(w_hbm, wf.at[y, x, z], in_sem.at[2])
    load_w.start()
    load_h.start()
    load_g.start()

    barrier = pltpu.get_barrier_semaphore()
    others = [near(a, s) for a in (0, 1) for s in steps]
    others += [at(x, y, lax.rem(z + r, 4)) for r in (1, 2, 3)]
    others += [{"group": peer(e)} for e in (1, 2, 3)]
    for other in others:
        pl.semaphore_signal(barrier, inc=1, device_id=other, device_id_type=pl.DeviceIdType.MESH)
    pl.semaphore_wait(barrier, len(others))

    def wz(r):
        return copy(w_hbm, wf.at[y, x, z], wz_ss.at[r - 1], wz_rs.at[r - 1], at(x, y, lax.rem(z + r, 4)))

    def gather(kind, r, hf, i):
        step = steps[i]
        zs = lax.rem(z + r, 4)
        cols = pl.ds(hf * HALF, HALF)
        first, second = hf, 1 - hf
        mine, across = (x, y) if hf == 0 else (y, x)
        prev = lax.rem(mine - step + 4, 4)
        back = lax.rem(across - step + 4, 4)
        if kind == 0:
            ref, axis = wf.at[y, x, zs, :, cols], first
        elif kind == 1:
            rows = pl.ds(i * (BLOCK // 2), BLOCK // 2)
            ref = wf.at[y, prev, zs, rows, cols] if hf == 0 else wf.at[prev, x, zs, rows, cols]
            axis = first
        elif kind == 2:
            ref = wf.at[y, :, zs, :, cols] if hf == 0 else wf.at[:, x, zs, :, cols]
            axis = second
        else:
            pair = pl.ds(2 * i, 2)
            ref = wf.at[back, pair, zs, :, cols] if hf == 0 else wf.at[pair, back, zs, :, cols]
            axis = second
        return copy(ref, ref, ag_ss.at[r, kind, hf, i], ag_rs.at[r, kind, hf, i], near(axis, step))

    def send_g():
        return copy(g_hbm, gr, ex_ss.at[CHUNKS], ex_rs.at[CHUNKS], zpair)

    def send_h(k):
        return copy(ht.at[1 - parity, k], htr.at[k], ex_ss.at[k], ex_rs.at[k], zpair)

    def chunk1(k, hf, dest, side):
        cols = pl.ds(hf * HALF, HALF)
        two = pl.ds(2 * side, 2)
        return part.at[k, two, dest, :, cols] if hf == 0 else part.at[k, dest, two, :, cols]

    def reduce1(kind, k, hf, i):
        step = steps[i]
        mine = x if hf == 0 else y
        if kind == 0:
            src, dst = chunk1(k, hf, lax.rem(mine + 2, 4), i), o1.at[k, hf, i]
        elif kind == 1:
            src, dst = chunk1(k, hf, lax.rem(mine + step + 4, 4), 1 - i), n1.at[k, hf, i]
        else:
            src, dst = o1.at[k, hf, i], s1.at[k, hf, i]
        return copy(src, dst, r1_ss.at[k, kind, hf, i], r1_rs.at[k, kind, hf, i], near(hf, step))

    def chunk2(k, hf, dest, side):
        return sums.at[k, hf, dest, pl.ds(side * ROWS, ROWS)]

    def reduce2(kind, k, hf, i):
        step = steps[i]
        mine = y if hf == 0 else x
        if kind == 0:
            src, dst = chunk2(k, hf, lax.rem(mine + 2, 4), i), o2.at[k, hf, i]
        elif kind == 1:
            src, dst = chunk2(k, hf, lax.rem(mine + step + 4, 4), 1 - i), n2.at[k, hf, i]
        else:
            src, dst = o2.at[k, hf, i], s2.at[k, hf, i]
        return copy(src, dst, r2_ss.at[k, kind, hf, i], r2_rs.at[k, kind, hf, i], near(1 - hf, step))

    def send_z(k):
        return copy(plane.at[k, 1 - level], zin.at[k], zz_ss.at[k], zz_rs.at[k], zcross)

    def send_inner(k, e):
        other = peer(e)
        return copy(
            inner.at[k, :, pl.ds(pl.multiple_of(other * QUARTER, QUARTER), QUARTER)],
            gin.at[k, e - 1], gi_ss.at[k, e - 1], gi_rs.at[k, e - 1], {"group": other},
        )

    def send_share(k, e):
        ref = share.at[k, :, pl.ds(pl.multiple_of(grp * QUARTER, QUARTER), QUARTER)]
        return copy(ref, ref, np_ss.at[k, e - 1], np_rs.at[k, e - 1], {"group": peer(e)})

    both = [(hf, i) for hf in (0, 1) for i in (0, 1)]

    def ga(r):
        for hf, i in both:
            gather(0, r, hf, i).start()

    def gb(r):
        for hf, i in both:
            gather(0, r, hf, i).wait_recv()
            gather(1, r, hf, i).start()

    def gc(r):
        for hf, i in both:
            gather(1, r, hf, i).wait_recv()
        for hf, i in both:
            gather(2, r, hf, i).start()

    def gd(r):
        for hf, i in both:
            gather(2, r, hf, i).wait_recv()
            gather(3, r, hf, i).start()

    def ge(r):
        for hf, i in both:
            gather(3, r, hf, i).wait_recv()

    def ra(k):
        @pl.loop(0, D // 256)
        def _(n):
            cols = pl.ds(pl.multiple_of(n * 256, 256), 256)
            mine = ht[parity, k].reshape(32 * ROWS, LOCAL)
            theirs = htr[k].reshape(32 * ROWS, LOCAL)
            total = jnp.dot(mine, g[:, cols], preferred_element_type=f32)
            total += jnp.dot(theirs, gr[:, cols], preferred_element_type=f32)
            part[k, :, :, :, cols] = total.reshape(4, 4, 2 * ROWS, 256)

        for kind in (0, 1):
            for hf, i in both:
                reduce1(kind, k, hf, i).start()

    def rb(k):
        for hf, i in both:
            mine = x if hf == 0 else y
            reduce1(0, k, hf, i).wait_recv()
            o1[k, hf, i] = o1[k, hf, i] + chunk1(k, hf, lax.rem(mine + steps[i] + 4, 4), i)[...]
            reduce1(2, k, hf, i).start()

    def rc(k):
        for hf in (0, 1):
            mine = x if hf == 0 else y
            for i in (0, 1):
                reduce1(1, k, hf, 1 - i).wait_recv()
                reduce1(2, k, hf, i).wait_recv()
                sums[k, hf, pl.ds(2 * i, 2)] = (chunk1(k, hf, mine, i)[...] + s1[k, hf, i]) + n1[k, hf, 1 - i]
        for kind in (0, 1):
            for hf, i in both:
                reduce2(kind, k, hf, i).start()

    def rd(k):
        for hf, i in both:
            mine = y if hf == 0 else x
            reduce2(0, k, hf, i).wait_recv()
            o2[k, hf, i] = o2[k, hf, i] + chunk2(k, hf, lax.rem(mine + steps[i] + 4, 4), i)[...]
            reduce2(2, k, hf, i).start()

    def re(k):
        for hf in (0, 1):
            mine = y if hf == 0 else x
            for i in (0, 1):
                reduce2(1, k, hf, 1 - i).wait_recv()
                reduce2(2, k, hf, i).wait_recv()
                plane[k, i, :, pl.ds(hf * HALF, HALF)] = (chunk2(k, hf, mine, i)[...] + s2[k, hf, i]) + n2[k, hf, 1 - i]
        send_z(k).start()

    def rf(k):
        send_z(k).wait_recv()
        rows = pl.ds(pl.multiple_of(k * ROWS, ROWS), ROWS)
        grad = (plane[k, level] + zin[k]) * (TOKENS ** (-0.5))
        first = beta_first * fm[rows, :].astype(f32) + (1.0 - beta_first) * grad
        second = beta_second * sm[rows, :].astype(f32) + (1.0 - beta_second) * grad * grad
        weight = wf[y, x, z, rows, :].astype(f32)
        nf_out[rows, :] = first.astype(bf16)
        ns_out[rows, :] = second.astype(bf16)
        inner[k] = weight - learn_rate * (first / (jnp.sqrt(second) + adam_eps) + decay_rate * weight)
        for e in (1, 2, 3):
            send_inner(k, e).start()

    def rg(k):
        rows = pl.ds(pl.multiple_of(k * ROWS, ROWS), ROWS)
        mine = pl.ds(pl.multiple_of(grp * QUARTER, QUARTER), QUARTER)
        total = inner[k, :, mine]
        for e in (1, 2, 3):
            send_inner(k, e).wait_recv()
            total += gin[k, e - 1]
        anchor = an[rows, :].astype(f32)
        pseudo = anchor - total / 4
        momentum = outer_beta * om[rows, :].astype(f32) + pseudo
        nm_out[rows, :] = momentum.astype(bf16)
        share[k, :, mine] = (anchor - outer_rate * (pseudo + outer_beta * momentum)).astype(bf16)
        for e in (1, 2, 3):
            send_share(k, e).start()

    def rh(k):
        for e in (1, 2, 3):
            send_share(k, e).wait_recv()
        np_out[pl.ds(pl.multiple_of(k * ROWS, ROWS), ROWS), :] = share[k]

    def out_lo(n):
        cols = pl.ds(pl.multiple_of(n * 256, 256), 256)
        return pltpu.make_async_copy(lo.at[:, cols], lo_hbm.at[:, cols], out_sem.at[0, n])

    def out_ig(n):
        cols = pl.ds(pl.multiple_of(n * 1024, 1024), 1024)
        return pltpu.make_async_copy(ig.at[:, cols], ig_hbm.at[:, cols], out_sem.at[1, n])

    def piece(n):
        cols = pl.ds(pl.multiple_of(n * 256, 256), 256)
        total = jnp.dot(h[...], wf[:, :, :, :, cols].reshape(FF, 256), preferred_element_type=f32)
        lo[:, cols] = (total * (FF ** (-0.5))).astype(bf16)
        out_lo(n).start()

        @pl.loop(0, 4)
        def _(c):
            units = pl.ds(pl.multiple_of(n * 1024 + c * 256, 256), 256)
            back = lax.dot_general(
                g[...], wf[n, c].reshape(256, D), (((1,), (1,)), ((), ())), preferred_element_type=f32
            )
            ig[:, units] = (back * (D ** (-0.5))).astype(bf16)

        out_ig(n).start()

    for r in (1, 2, 3):
        wz(r).start()
    load_w.wait()
    ga(0)
    load_h.wait()

    @pl.loop(0, 32)
    def _(n):
        d, m = n // 2, lax.rem(n, 2)
        turned = h[:, pl.ds(pl.multiple_of(n * 128, 128), 128)].T
        for par in (0, 1):
            ht[par, :, d, m] = turned[par * BLOCK : (par + 1) * BLOCK].reshape(CHUNKS, ROWS, LOCAL)

    gb(0)
    send_g().start()
    load_g.wait()

    @pl.loop(0, 4)
    def _(r):
        @pl.when(r < 3)
        def _():
            copy(w_hbm, wf.at[y, x, z], wz_ss.at[2 - r], wz_rs.at[2 - r], zpair).wait_recv()
            ga(r + 1)

        gc(r)
        send_h(r).start()

        @pl.when(r < 3)
        def _():
            gb(r + 1)

        gd(r)

    @pl.loop(0, 4)
    def _(r):
        ge(r)

    send_g().wait_recv()

    @pl.loop(0, CHUNKS + 4)
    def _(t):
        @pl.when(t < CHUNKS)
        def _():
            send_h(t).wait_recv()
            ra(t)

        @pl.when((t >= 1) & (t < CHUNKS + 1))
        def _():
            rc(t - 1)

        @pl.when((t >= 2) & (t < CHUNKS + 2))
        def _():
            rf(t - 2)

        @pl.when(t < CHUNKS)
        def _():
            piece(t)
            rb(t)

        @pl.when((t >= 1) & (t < CHUNKS + 1))
        def _():
            rd(t - 1)

        @pl.when((t >= 3) & (t < CHUNKS + 3))
        def _():
            rg(t - 3)

        @pl.when((t >= 1) & (t < CHUNKS + 1))
        def _():
            re(t - 1)

        @pl.when(t >= 4)
        def _():
            rh(t - 4)

    for r in (1, 2, 3):
        wz(r).wait_send()
    send_g().wait_send()

    @pl.loop(0, 4)
    def _(k):
        for hf, i in both:
            for kind in range(4):
                gather(kind, k, hf, i).wait_send()
            for kind in range(3):
                reduce1(kind, k, hf, i).wait_send()
                reduce2(kind, k, hf, i).wait_send()
        send_h(k).wait_send()
        send_z(k).wait_send()
        for e in (1, 2, 3):
            send_inner(k, e).wait_send()
            send_share(k, e).wait_send()
        out_lo(k).wait()
        out_ig(k).wait()


def local(hidden_rows, out_grad, params, first_moment, second_moment, anchor, outer_momentum):
    anywhere = pl.BlockSpec(memory_space=pl.ANY)
    vmem = pl.BlockSpec(memory_space=pltpu.VMEM)
    dma = pltpu.SemaphoreType.DMA
    n = CHUNKS
    step1 = pltpu.VMEM((n, 2, 2, 2, 2 * ROWS, HALF), f32)
    step2 = pltpu.VMEM((n, 2, 2, ROWS, HALF), f32)

    def pair(*shape):
        return [dma(shape), dma(shape)]

    out = pl.pallas_call(
        kernel,
        out_shape=[
            jax.ShapeDtypeStruct((LOCAL, D), bf16),
            jax.ShapeDtypeStruct((LOCAL, FF), bf16),
            jax.ShapeDtypeStruct((BLOCK, D), bf16),
            jax.ShapeDtypeStruct((BLOCK, D), bf16),
            jax.ShapeDtypeStruct((BLOCK, D), bf16),
            jax.ShapeDtypeStruct((BLOCK, QUARTER), bf16),
        ],
        in_specs=[anywhere] * 3 + [vmem] * 4,
        out_specs=[anywhere] * 2 + [vmem] * 4,
        scratch_shapes=[
            pltpu.VMEM((LOCAL, FF), bf16),
            pltpu.VMEM((LOCAL, D), bf16),
            pltpu.VMEM((LOCAL, D), bf16),
            pltpu.VMEM((4, 4, 4, BLOCK, D), bf16),
            pltpu.VMEM((2, n, 16, 2, ROWS, LOCAL), bf16),
            pltpu.VMEM((n, 16, 2, ROWS, LOCAL), bf16),
            pltpu.VMEM((n, 4, 4, 2 * ROWS, D), f32),
            step1, step1, step1,
            pltpu.VMEM((n, 2, 4, 2 * ROWS, HALF), f32),
            step2, step2, step2,
            pltpu.VMEM((n, 2, ROWS, D), f32),
            pltpu.VMEM((n, ROWS, D), f32),
            pltpu.VMEM((n, ROWS, D), f32),
            pltpu.VMEM((n, 3, ROWS, QUARTER), f32),
            pltpu.VMEM((n, ROWS, D), bf16),
            pltpu.VMEM((LOCAL, D), bf16),
            pltpu.VMEM((LOCAL, FF), bf16),
            dma((3,)),
            dma((2, 4)),
            *pair(3),
            *pair(4, 4, 2, 2),
            *pair(n + 1),
            *pair(n, 3, 2, 2),
            *pair(n, 3, 2, 2),
            *pair(n),
            *pair(n, 3),
            *pair(n, 3),
        ],
        compiler_params=pltpu.CompilerParams(
            collective_id=0, has_side_effects=True, vmem_limit_bytes=60 * MIB
        ),
        cost_estimate=pl.CostEstimate(flops=13 * 10**9, bytes_accessed=13 * MIB, transcendentals=0),
        name="step",
    )(hidden_rows[0], out_grad[0], params[0], first_moment[0], second_moment[0], anchor, outer_momentum)
    return (out[0][None], out[1][None], out[2], out[3][None], out[4][None], out[5])


def solution(mesh):
    rows = P("group", "fsdp", None)
    return jax.shard_map(
        local,
        mesh=mesh,
        in_specs=(rows, rows, rows, rows, rows, P("fsdp", "group"), P("fsdp", "group")),
        out_specs=(rows, rows, P("fsdp", None), rows, rows, P("fsdp", "group")),
        check_vma=False,
    )
```

```python
import jax
import jax.numpy as jnp
from jax import lax
from jax.experimental import pallas as pl
from jax.experimental.pallas import tpu as pltpu
from jax.sharding import PartitionSpec as P

D = 1024
FF = 4096
TOKENS = 32768
BLOCK = 64
LOCAL = 512
CHUNKS = 4
ROWS = BLOCK // CHUNKS
HALF = D // 2
QUARTER = D // 4
MIB = 1 << 20

beta_first = 0.9
beta_second = 0.95
adam_eps = 1e-08
learn_rate = 0.1
decay_rate = 0.1
outer_rate = 0.7
outer_beta = 0.9

bf16 = jnp.bfloat16
f32 = jnp.float32


def kernel(
    h_hbm, g_hbm, w_hbm, fm, sm, an, om,
    lo, ig, np_out, nf_out, ns_out, nm_out,
    h, g, gr, wf, ht, htr, part, o1, n1, s1, sums, o2, n2, s2, plane, zin,
    inner, inner_in, both_sum, both_in, anchors, momenta, moved, share,
    in_sem,
    wz_ss, wz_rs, ag_ss, ag_rs, ex_ss, ex_rs, r1_ss, r1_rs, r2_ss, r2_rs, zz_ss, zz_rs,
    am_ss, am_rs, gi_ss, gi_rs, gh_ss, gh_rs, np_ss, np_rs,
):
    me = lax.axis_index("fsdp")
    grp = lax.axis_index("group")
    z, x, y = lax.rem(me, 4), lax.rem(me // 4, 4), me // 16
    parity, level = lax.rem(z, 2), z // 2

    def at(xx, yy, zz):
        return {"fsdp": (yy * 4 + xx) * 4 + zz}

    def near(axis, step):
        if axis == 0:
            return at(lax.rem(x + step + 4, 4), y, z)
        return at(x, lax.rem(y + step + 4, 4), z)

    core, high = lax.rem(grp, 2), grp // 2
    other_core = {"group": high * 2 + 1 - core}
    other_half = {"group": (1 - high) * 2 + core}

    def copy(src, dst, ss, rs, device):
        return pltpu.make_async_remote_copy(
            src_ref=src, dst_ref=dst, send_sem=ss, recv_sem=rs, device_id=device, device_id_type=pl.DeviceIdType.MESH
        )

    zpair = at(x, y, z + 1 - 2 * parity)
    zcross = at(x, y, lax.rem(z + 2, 4))
    steps = (1, -1)

    load_g = pltpu.make_async_copy(g_hbm, g, in_sem.at[0])
    load_h = pltpu.make_async_copy(h_hbm, h, in_sem.at[1])
    load_w = pltpu.make_async_copy(w_hbm, wf.at[y, x, z], in_sem.at[2])
    load_w.start()
    load_h.start()
    load_g.start()

    barrier = pltpu.get_barrier_semaphore()
    others = [near(a, s) for a in (0, 1) for s in steps]
    others += [at(x, y, lax.rem(z + r, 4)) for r in (1, 2, 3)]
    others += [other_core, other_half]
    for other in others:
        pl.semaphore_signal(barrier, inc=1, device_id=other, device_id_type=pl.DeviceIdType.MESH)
    pl.semaphore_wait(barrier, len(others))

    def wz(r):
        return copy(w_hbm, wf.at[y, x, z], wz_ss.at[r - 1], wz_rs.at[r - 1], at(x, y, lax.rem(z + r, 4)))

    def gather(kind, r, hf, i):
        step = steps[i]
        zs = lax.rem(z + r, 4)
        cols = pl.ds(hf * HALF, HALF)
        first, second = hf, 1 - hf
        mine, across = (x, y) if hf == 0 else (y, x)
        prev = lax.rem(mine - step + 4, 4)
        back = lax.rem(across - step + 4, 4)
        if kind == 0:
            ref, axis = wf.at[y, x, zs, :, cols], first
        elif kind == 1:
            rows = pl.ds(i * (BLOCK // 2), BLOCK // 2)
            ref = wf.at[y, prev, zs, rows, cols] if hf == 0 else wf.at[prev, x, zs, rows, cols]
            axis = first
        elif kind == 2:
            ref = wf.at[y, :, zs, :, cols] if hf == 0 else wf.at[:, x, zs, :, cols]
            axis = second
        else:
            pair = pl.ds(2 * i, 2)
            ref = wf.at[back, pair, zs, :, cols] if hf == 0 else wf.at[pair, back, zs, :, cols]
            axis = second
        return copy(ref, ref, ag_ss.at[r, kind, hf, i], ag_rs.at[r, kind, hf, i], near(axis, step))

    def send_g():
        return copy(g_hbm, gr, ex_ss.at[CHUNKS], ex_rs.at[CHUNKS], zpair)

    def send_h(k):
        return copy(ht.at[1 - parity, k], htr.at[k], ex_ss.at[k], ex_rs.at[k], zpair)

    def chunk1(k, hf, dest, side):
        cols = pl.ds(hf * HALF, HALF)
        two = pl.ds(2 * side, 2)
        return part.at[k, two, dest, :, cols] if hf == 0 else part.at[k, dest, two, :, cols]

    def reduce1(kind, k, hf, i):
        step = steps[i]
        mine = x if hf == 0 else y
        if kind == 0:
            src, dst = chunk1(k, hf, lax.rem(mine + 2, 4), i), o1.at[k, hf, i]
        elif kind == 1:
            src, dst = chunk1(k, hf, lax.rem(mine + step + 4, 4), 1 - i), n1.at[k, hf, i]
        else:
            src, dst = o1.at[k, hf, i], s1.at[k, hf, i]
        return copy(src, dst, r1_ss.at[k, kind, hf, i], r1_rs.at[k, kind, hf, i], near(hf, step))

    def chunk2(k, hf, dest, side):
        return sums.at[k, hf, dest, pl.ds(side * ROWS, ROWS)]

    def reduce2(kind, k, hf, i):
        step = steps[i]
        mine = y if hf == 0 else x
        if kind == 0:
            src, dst = chunk2(k, hf, lax.rem(mine + 2, 4), i), o2.at[k, hf, i]
        elif kind == 1:
            src, dst = chunk2(k, hf, lax.rem(mine + step + 4, 4), 1 - i), n2.at[k, hf, i]
        else:
            src, dst = o2.at[k, hf, i], s2.at[k, hf, i]
        return copy(src, dst, r2_ss.at[k, kind, hf, i], r2_rs.at[k, kind, hf, i], near(1 - hf, step))

    def send_z(k):
        return copy(plane.at[k, 1 - level], zin.at[k], zz_ss.at[k], zz_rs.at[k], zcross)

    def send_anchor():
        return copy(an, anchors.at[high], am_ss.at[0], am_rs.at[0], other_half)

    def send_momentum():
        return copy(om, momenta.at[high], am_ss.at[1], am_rs.at[1], other_half)

    def send_inner(k):
        return copy(inner.at[k, :, 1 - core], inner_in.at[k], gi_ss.at[k], gi_rs.at[k], other_core)

    def send_both(k):
        return copy(both_sum.at[k], both_in.at[k], gh_ss.at[k], gh_rs.at[k], other_half)

    def send_share(k):
        ref = share.at[k, :, core]
        return copy(ref, ref, np_ss.at[k], np_rs.at[k], other_core)

    both = [(hf, i) for hf in (0, 1) for i in (0, 1)]

    def ga(r):
        for hf, i in both:
            gather(0, r, hf, i).start()

    def gb(r):
        for hf, i in both:
            gather(0, r, hf, i).wait_recv()
            gather(1, r, hf, i).start()

    def gc(r):
        for hf, i in both:
            gather(1, r, hf, i).wait_recv()
        for hf, i in both:
            gather(2, r, hf, i).start()

    def gd(r):
        for hf, i in both:
            gather(2, r, hf, i).wait_recv()
            gather(3, r, hf, i).start()

    def ge(r):
        for hf, i in both:
            gather(3, r, hf, i).wait_recv()

    def ra(k):
        @pl.loop(0, D // 256)
        def _(n):
            cols = pl.ds(pl.multiple_of(n * 256, 256), 256)
            mine = ht[parity, k].reshape(32 * ROWS, LOCAL)
            theirs = htr[k].reshape(32 * ROWS, LOCAL)
            total = jnp.dot(mine, g[:, cols], preferred_element_type=f32)
            total += jnp.dot(theirs, gr[:, cols], preferred_element_type=f32)
            part[k, :, :, :, cols] = total.reshape(4, 4, 2 * ROWS, 256)

        for kind in (0, 1):
            for hf, i in both:
                reduce1(kind, k, hf, i).start()

    def rb(k):
        for hf, i in both:
            mine = x if hf == 0 else y
            reduce1(0, k, hf, i).wait_recv()
            o1[k, hf, i] = o1[k, hf, i] + chunk1(k, hf, lax.rem(mine + steps[i] + 4, 4), i)[...]
            reduce1(2, k, hf, i).start()

    def rc(k):
        for hf in (0, 1):
            mine = x if hf == 0 else y
            for i in (0, 1):
                reduce1(1, k, hf, 1 - i).wait_recv()
                reduce1(2, k, hf, i).wait_recv()
                sums[k, hf, pl.ds(2 * i, 2)] = (chunk1(k, hf, mine, i)[...] + s1[k, hf, i]) + n1[k, hf, 1 - i]
        for kind in (0, 1):
            for hf, i in both:
                reduce2(kind, k, hf, i).start()

    def rd(k):
        for hf, i in both:
            mine = y if hf == 0 else x
            reduce2(0, k, hf, i).wait_recv()
            o2[k, hf, i] = o2[k, hf, i] + chunk2(k, hf, lax.rem(mine + steps[i] + 4, 4), i)[...]
            reduce2(2, k, hf, i).start()

    def re(k):
        for hf in (0, 1):
            mine = y if hf == 0 else x
            for i in (0, 1):
                reduce2(1, k, hf, 1 - i).wait_recv()
                reduce2(2, k, hf, i).wait_recv()
                plane[k, i, :, pl.ds(hf * HALF, HALF)] = (chunk2(k, hf, mine, i)[...] + s2[k, hf, i]) + n2[k, hf, 1 - i]
        send_z(k).start()

    def rf(k):
        send_z(k).wait_recv()
        rows = pl.ds(pl.multiple_of(k * ROWS, ROWS), ROWS)
        grad = (plane[k, level] + zin[k]) * (TOKENS ** (-0.5))
        first = beta_first * fm[rows, :].astype(f32) + (1.0 - beta_first) * grad
        second = beta_second * sm[rows, :].astype(f32) + (1.0 - beta_second) * grad * grad
        weight = wf[y, x, z, rows, :].astype(f32)
        nf_out[rows, :] = first.astype(bf16)
        ns_out[rows, :] = second.astype(bf16)
        fresh = weight - learn_rate * (first / (jnp.sqrt(second) + adam_eps) + decay_rate * weight)
        for q in range(4):
            inner[k, q // 2, q % 2] = fresh[:, q * QUARTER : (q + 1) * QUARTER]
        send_inner(k).start()

    def rg(k):
        send_inner(k).wait_recv()
        both_sum[k] = inner[k, :, core] + inner_in[k]
        send_both(k).start()

    def rh(k):
        send_both(k).wait_recv()
        rows = pl.ds(pl.multiple_of(k * ROWS, ROWS), ROWS)
        anchor = anchors[:, rows].astype(f32)
        pseudo = anchor - (both_sum[k] + both_in[k]) / 4
        momentum = outer_beta * momenta[:, rows].astype(f32) + pseudo
        moved[...] = momentum.astype(bf16)
        nm_out[rows, :] = moved[high]
        share[k, :, core] = (anchor - outer_rate * (pseudo + outer_beta * momentum)).astype(bf16)
        send_share(k).start()

    def ri(k):
        send_share(k).wait_recv()
        rows = pl.ds(pl.multiple_of(k * ROWS, ROWS), ROWS)
        for q in range(4):
            np_out[rows, q * QUARTER : (q + 1) * QUARTER] = share[k, q // 2, q % 2]

    def forward(n):
        cols = pl.ds(pl.multiple_of(n * 256, 256), 256)
        total = jnp.dot(h[...], wf[:, :, :, :, cols].reshape(FF, 256), preferred_element_type=f32)
        lo[:, cols] = (total * (FF ** (-0.5))).astype(bf16)
    def backward(n):
        @pl.loop(0, 4)
        def _(c):
            units = pl.ds(pl.multiple_of(n * 1024 + c * 256, 256), 256)
            back = lax.dot_general(
                g[...], wf[n, c].reshape(256, D), (((1,), (1,)), ((), ())), preferred_element_type=f32
            )
            ig[:, units] = (back * (D ** (-0.5))).astype(bf16)

    def shard_in(r):
        copy(w_hbm, wf.at[y, x, z], wz_ss.at[3 - r], wz_rs.at[3 - r], zpair).wait_recv()

    for r in (1, 3, 2):
        wz(r).start()
    send_g().start()
    load_w.wait()
    ga(0)
    load_h.wait()

    @pl.loop(0, 32)
    def _(n):
        d, m = n // 2, lax.rem(n, 2)
        turned = h[:, pl.ds(pl.multiple_of(n * 128, 128), 128)].T
        for par in (0, 1):
            ht[par, :, d, m] = turned[par * BLOCK : (par + 1) * BLOCK].reshape(CHUNKS, ROWS, LOCAL)

    @pl.loop(0, CHUNKS)
    def _(k):
        send_h(k).start()

    send_anchor().start()
    send_momentum().start()
    anchors[high] = an[...]
    momenta[high] = om[...]

    load_g.wait()
    gb(0)
    shard_in(1)
    ga(1)

    @pl.loop(0, 4)
    def _(r):
        gc(r)

        @pl.when(r < 2)
        def _():
            shard_in(r + 2)
            ga(r + 2)

        @pl.when(r < 3)
        def _():
            gb(r + 1)
            gd(r)

    @pl.loop(0, CHUNKS + 4)
    def _(t):
        @pl.when(t == 0)
        def _():
            send_g().wait_recv()

        @pl.when(t < CHUNKS)
        def _():
            send_h(t).wait_recv()
            ra(t)

        @pl.when((t >= 1) & (t < CHUNKS + 1))
        def _():
            rd(t - 1)

        @pl.when(t == 0)
        def _():
            gd(3)

            @pl.loop(0, 4)
            def _(r):
                ge(r)

        @pl.when((t >= 2) & (t < CHUNKS + 2))
        def _():
            rf(t - 2)

        @pl.when(t < CHUNKS)
        def _():
            forward(t)
            rb(t)
            backward(t)

        @pl.when((t >= 2) & (t < CHUNKS + 2))
        def _():
            rg(t - 2)

        @pl.when((t >= 1) & (t < CHUNKS + 1))
        def _():
            re(t - 1)

        @pl.when(t == 3)
        def _():
            send_anchor().wait_recv()
            send_momentum().wait_recv()

        @pl.when((t >= 3) & (t < CHUNKS + 3))
        def _():
            rh(t - 3)

        @pl.when(t < CHUNKS)
        def _():
            rc(t)

        @pl.when(t >= 4)
        def _():
            ri(t - 4)

    for r in (1, 2, 3):
        wz(r).wait_send()
    send_g().wait_send()
    send_anchor().wait_send()
    send_momentum().wait_send()

    @pl.loop(0, 4)
    def _(k):
        for hf, i in both:
            for kind in range(4):
                gather(kind, k, hf, i).wait_send()
            for kind in range(3):
                reduce1(kind, k, hf, i).wait_send()
                reduce2(kind, k, hf, i).wait_send()
        send_h(k).wait_send()
        send_z(k).wait_send()
        send_inner(k).wait_send()
        send_both(k).wait_send()
        send_share(k).wait_send()


def local(hidden_rows, out_grad, params, first_moment, second_moment, anchor, outer_momentum):
    shapes = [(LOCAL, D), (LOCAL, FF), (BLOCK, D), (BLOCK, D), (BLOCK, D), (BLOCK, QUARTER)]
    anywhere = pl.BlockSpec(memory_space=pl.ANY)
    vmem = pl.BlockSpec(memory_space=pltpu.VMEM)
    dma = pltpu.SemaphoreType.DMA
    n = CHUNKS
    step1 = pltpu.VMEM((n, 2, 2, 2, 2 * ROWS, HALF), f32)
    step2 = pltpu.VMEM((n, 2, 2, ROWS, HALF), f32)

    quarters = pltpu.VMEM((n, 2, ROWS, QUARTER), f32)

    def pair(*shape):
        return [dma(shape), dma(shape)]

    out = pl.pallas_call(
        kernel,
        out_shape=[pltpu.VMEM(shape, bf16) for shape in shapes],
        in_specs=[anywhere] * 3 + [vmem] * 4,
        out_specs=[vmem] * 6,
        scratch_shapes=[
            pltpu.VMEM((LOCAL, FF), bf16),
            pltpu.VMEM((LOCAL, D), bf16),
            pltpu.VMEM((LOCAL, D), bf16),
            pltpu.VMEM((4, 4, 4, BLOCK, D), bf16),
            pltpu.VMEM((2, n, 16, 2, ROWS, LOCAL), bf16),
            pltpu.VMEM((n, 16, 2, ROWS, LOCAL), bf16),
            pltpu.VMEM((n, 4, 4, 2 * ROWS, D), f32),
            step1, step1, step1,
            pltpu.VMEM((n, 2, 4, 2 * ROWS, HALF), f32),
            step2, step2, step2,
            pltpu.VMEM((n, 2, ROWS, D), f32),
            pltpu.VMEM((n, ROWS, D), f32),
            pltpu.VMEM((n, 2, 2, ROWS, QUARTER), f32),
            quarters, quarters, quarters,
            pltpu.VMEM((2, BLOCK, QUARTER), bf16),
            pltpu.VMEM((2, BLOCK, QUARTER), bf16),
            pltpu.VMEM((2, ROWS, QUARTER), bf16),
            pltpu.VMEM((n, 2, 2, ROWS, QUARTER), bf16),
            dma((3,)),
            *pair(3),
            *pair(4, 4, 2, 2),
            *pair(n + 1),
            *pair(n, 3, 2, 2),
            *pair(n, 3, 2, 2),
            *pair(n),
            *pair(2),
            *pair(n),
            *pair(n),
            *pair(n),
        ],
        compiler_params=pltpu.CompilerParams(
            collective_id=0, has_side_effects=True, vmem_limit_bytes=50 * MIB
        ),
        cost_estimate=pl.CostEstimate(flops=13 * 10**9, bytes_accessed=13 * MIB, transcendentals=0),
        name="step",
    )(hidden_rows[0], out_grad[0], params[0], first_moment[0], second_moment[0], anchor, outer_momentum)
    return (out[0][None], out[1][None], out[2], out[3][None], out[4][None], out[5])


def solution(mesh):
    rows = P("group", "fsdp", None)
    return jax.shard_map(
        local,
        mesh=mesh,
        in_specs=(rows, rows, rows, rows, rows, P("fsdp", "group"), P("fsdp", "group")),
        out_specs=(rows, rows, P("fsdp", None), rows, rows, P("fsdp", "group")),
        check_vma=False,
    )
```

```python
import jax
import jax.numpy as jnp
from jax import lax
from jax.experimental import pallas as pl
from jax.experimental.pallas import tpu as pltpu
from jax.sharding import PartitionSpec as P

D = 1024
FF = 4096
TOKENS = 32768
BLOCK = 64
LOCAL = 512
CHUNKS = 4
ROWS = BLOCK // CHUNKS
HALF = D // 2
QUARTER = D // 4
MIB = 1 << 20

beta_first = 0.9
beta_second = 0.95
adam_eps = 1e-08
learn_rate = 0.1
decay_rate = 0.1
outer_rate = 0.7
outer_beta = 0.9

bf16 = jnp.bfloat16
f32 = jnp.float32


def kernel(
    h_hbm, g_hbm, w_hbm, fm_hbm, sm_hbm, an_hbm, om_hbm,
    lo, ig, np_out, nf_out, ns_out, nm_out,
    h, g, fm, sm, gr, wf, ht, htr, part, o1, n1, s1, sums, o2, n2, s2, plane, zin,
    inner, inner_in, both_sum, both_in, anchors, momenta, moved, share,
    in_sem,
    wz_ss, wz_rs, ag_ss, ag_rs, ex_ss, ex_rs, r1_ss, r1_rs, r2_ss, r2_rs, zz_ss, zz_rs,
    am_ss, am_rs, gi_ss, gi_rs, gh_ss, gh_rs, np_ss, np_rs,
):
    me = lax.axis_index("fsdp")
    grp = lax.axis_index("group")
    z, x, y = lax.rem(me, 4), lax.rem(me // 4, 4), me // 16
    parity, level = lax.rem(z, 2), z // 2

    def at(xx, yy, zz):
        return {"fsdp": (yy * 4 + xx) * 4 + zz}

    def near(axis, step):
        if axis == 0:
            return at(lax.rem(x + step + 4, 4), y, z)
        return at(x, lax.rem(y + step + 4, 4), z)

    core, high = lax.rem(grp, 2), grp // 2
    other_core = {"group": high * 2 + 1 - core}
    other_half = {"group": (1 - high) * 2 + core}

    def copy(src, dst, ss, rs, device):
        return pltpu.make_async_remote_copy(
            src_ref=src, dst_ref=dst, send_sem=ss, recv_sem=rs, device_id=device, device_id_type=pl.DeviceIdType.MESH
        )

    zpair = at(x, y, z + 1 - 2 * parity)
    zcross = at(x, y, lax.rem(z + 2, 4))
    steps = (1, -1)

    load_g = pltpu.make_async_copy(g_hbm, g, in_sem.at[0])
    load_h = pltpu.make_async_copy(h_hbm, h, in_sem.at[1])
    load_w = pltpu.make_async_copy(w_hbm, wf.at[y, x, z], in_sem.at[2])
    load_w.start()
    load_h.start()
    load_g.start()
    load_small = [
        pltpu.make_async_copy(src, dst, in_sem.at[3 + j])
        for j, (src, dst) in enumerate(
            ((fm_hbm, fm), (sm_hbm, sm), (an_hbm, anchors.at[high]), (om_hbm, momenta.at[high]))
        )
    ]
    for load in load_small:
        load.start()

    barrier = pltpu.get_barrier_semaphore()
    others = [near(a, s) for a in (0, 1) for s in steps]
    others += [at(x, y, lax.rem(z + r, 4)) for r in (1, 2, 3)]
    others += [other_core, other_half]
    for other in others:
        pl.semaphore_signal(barrier, inc=1, device_id=other, device_id_type=pl.DeviceIdType.MESH)
    pl.semaphore_wait(barrier, len(others))

    def wz(r):
        return copy(w_hbm, wf.at[y, x, z], wz_ss.at[r - 1], wz_rs.at[r - 1], at(x, y, lax.rem(z + r, 4)))

    def gather(kind, r, hf, i):
        step = steps[i]
        zs = lax.rem(z + r, 4)
        cols = pl.ds(hf * HALF, HALF)
        first, second = hf, 1 - hf
        mine, across = (x, y) if hf == 0 else (y, x)
        prev = lax.rem(mine - step + 4, 4)
        back = lax.rem(across - step + 4, 4)
        if kind == 0:
            ref, axis = wf.at[y, x, zs, :, cols], first
        elif kind == 1:
            rows = pl.ds(i * (BLOCK // 2), BLOCK // 2)
            ref = wf.at[y, prev, zs, rows, cols] if hf == 0 else wf.at[prev, x, zs, rows, cols]
            axis = first
        elif kind == 2:
            ref = wf.at[y, :, zs, :, cols] if hf == 0 else wf.at[:, x, zs, :, cols]
            axis = second
        else:
            pair = pl.ds(2 * i, 2)
            ref = wf.at[back, pair, zs, :, cols] if hf == 0 else wf.at[pair, back, zs, :, cols]
            axis = second
        return copy(ref, ref, ag_ss.at[r, kind, hf, i], ag_rs.at[r, kind, hf, i], near(axis, step))

    def send_g():
        return copy(g_hbm, gr, ex_ss.at[CHUNKS], ex_rs.at[CHUNKS], zpair)

    def send_h(k):
        return copy(ht.at[1 - parity, k], htr.at[k], ex_ss.at[k], ex_rs.at[k], zpair)

    def chunk1(k, hf, dest, side):
        cols = pl.ds(hf * HALF, HALF)
        two = pl.ds(2 * side, 2)
        return part.at[k, two, dest, :, cols] if hf == 0 else part.at[k, dest, two, :, cols]

    def reduce1(kind, k, hf, i):
        step = steps[i]
        mine = x if hf == 0 else y
        if kind == 0:
            src, dst = chunk1(k, hf, lax.rem(mine + 2, 4), i), o1.at[k, hf, i]
        elif kind == 1:
            src, dst = chunk1(k, hf, lax.rem(mine + step + 4, 4), 1 - i), n1.at[k, hf, i]
        else:
            src, dst = o1.at[k, hf, i], s1.at[k, hf, i]
        return copy(src, dst, r1_ss.at[k, kind, hf, i], r1_rs.at[k, kind, hf, i], near(hf, step))

    def chunk2(k, hf, dest, side):
        return sums.at[k, hf, dest, pl.ds(side * ROWS, ROWS)]

    def reduce2(kind, k, hf, i):
        step = steps[i]
        mine = y if hf == 0 else x
        if kind == 0:
            src, dst = chunk2(k, hf, lax.rem(mine + 2, 4), i), o2.at[k, hf, i]
        elif kind == 1:
            src, dst = chunk2(k, hf, lax.rem(mine + step + 4, 4), 1 - i), n2.at[k, hf, i]
        else:
            src, dst = o2.at[k, hf, i], s2.at[k, hf, i]
        return copy(src, dst, r2_ss.at[k, kind, hf, i], r2_rs.at[k, kind, hf, i], near(1 - hf, step))

    def send_z(k):
        return copy(plane.at[k, 1 - level], zin.at[k], zz_ss.at[k], zz_rs.at[k], zcross)

    def send_anchor():
        return copy(an_hbm, anchors.at[high], am_ss.at[0], am_rs.at[0], other_half)

    def send_momentum():
        return copy(om_hbm, momenta.at[high], am_ss.at[1], am_rs.at[1], other_half)

    def send_inner(k):
        return copy(inner.at[k, :, 1 - core], inner_in.at[k], gi_ss.at[k], gi_rs.at[k], other_core)

    def send_both(k):
        return copy(both_sum.at[k], both_in.at[k], gh_ss.at[k], gh_rs.at[k], other_half)

    def send_share(k):
        ref = share.at[k, :, core]
        return copy(ref, ref, np_ss.at[k], np_rs.at[k], other_core)

    both = [(hf, i) for hf in (0, 1) for i in (0, 1)]

    def ga(r):
        for hf, i in both:
            gather(0, r, hf, i).start()

    def gb(r):
        for hf, i in both:
            gather(0, r, hf, i).wait_recv()
            gather(1, r, hf, i).start()

    def gc(r):
        for hf, i in both:
            gather(1, r, hf, i).wait_recv()
        for hf, i in both:
            gather(2, r, hf, i).start()

    def gd(r):
        for hf, i in both:
            gather(2, r, hf, i).wait_recv()
            gather(3, r, hf, i).start()

    def ge(r):
        for hf, i in both:
            gather(3, r, hf, i).wait_recv()

    def own(k):
        @pl.loop(0, D // 256)
        def _(n):
            cols = pl.ds(pl.multiple_of(n * 256, 256), 256)
            mine = ht[parity, k].reshape(32 * ROWS, LOCAL)
            total = jnp.dot(mine, g[:, cols], preferred_element_type=f32)
            part[k, :, :, :, cols] = total.reshape(4, 4, 2 * ROWS, 256)

    def ra(k):
        @pl.loop(0, 2)
        def _(hf):
            @pl.loop(0, 2)
            def _(n):
                cols = pl.ds(pl.multiple_of(hf * HALF + n * 256, 256), 256)
                theirs = htr[k].reshape(32 * ROWS, LOCAL)
                total = jnp.dot(theirs, gr[:, cols], preferred_element_type=f32)
                part[k, :, :, :, cols] += total.reshape(4, 4, 2 * ROWS, 256)

            for half in (0, 1):

                @pl.when(hf == half)
                def _():
                    for kind in (0, 1):
                        for i in (0, 1):
                            reduce1(kind, k, half, i).start()

    def rb(k):
        for hf, i in both:
            mine = x if hf == 0 else y
            reduce1(0, k, hf, i).wait_recv()
            o1[k, hf, i] = o1[k, hf, i] + chunk1(k, hf, lax.rem(mine + steps[i] + 4, 4), i)[...]
            reduce1(2, k, hf, i).start()

    def rc(k):
        for hf in (0, 1):
            mine = x if hf == 0 else y
            for i in (0, 1):
                reduce1(1, k, hf, 1 - i).wait_recv()
                reduce1(2, k, hf, i).wait_recv()
                sums[k, hf, pl.ds(2 * i, 2)] = (chunk1(k, hf, mine, i)[...] + s1[k, hf, i]) + n1[k, hf, 1 - i]
        for kind in (0, 1):
            for hf, i in both:
                reduce2(kind, k, hf, i).start()

    def rd(k):
        for hf, i in both:
            mine = y if hf == 0 else x
            reduce2(0, k, hf, i).wait_recv()
            o2[k, hf, i] = o2[k, hf, i] + chunk2(k, hf, lax.rem(mine + steps[i] + 4, 4), i)[...]
            reduce2(2, k, hf, i).start()

    def re(k):
        for hf in (0, 1):
            mine = y if hf == 0 else x
            for i in (0, 1):
                reduce2(1, k, hf, 1 - i).wait_recv()
                reduce2(2, k, hf, i).wait_recv()
                plane[k, i, :, pl.ds(hf * HALF, HALF)] = (chunk2(k, hf, mine, i)[...] + s2[k, hf, i]) + n2[k, hf, 1 - i]
        send_z(k).start()

    def rf(k):
        send_z(k).wait_recv()
        rows = pl.ds(pl.multiple_of(k * ROWS, ROWS), ROWS)
        grad = (plane[k, level] + zin[k]) * (TOKENS ** (-0.5))
        first = beta_first * fm[rows, :].astype(f32) + (1.0 - beta_first) * grad
        second = beta_second * sm[rows, :].astype(f32) + (1.0 - beta_second) * grad * grad
        weight = wf[y, x, z, rows, :].astype(f32)
        nf_out[rows, :] = first.astype(bf16)
        ns_out[rows, :] = second.astype(bf16)
        fresh = weight - learn_rate * (first / (jnp.sqrt(second) + adam_eps) + decay_rate * weight)
        for q in range(4):
            inner[k, q // 2, q % 2] = fresh[:, q * QUARTER : (q + 1) * QUARTER]
        send_inner(k).start()

    def rg(k):
        send_inner(k).wait_recv()
        both_sum[k] = inner[k, :, core] + inner_in[k]
        send_both(k).start()

    def rh(k):
        send_both(k).wait_recv()
        rows = pl.ds(pl.multiple_of(k * ROWS, ROWS), ROWS)
        anchor = anchors[:, rows].astype(f32)
        pseudo = anchor - (both_sum[k] + both_in[k]) / 4
        momentum = outer_beta * momenta[:, rows].astype(f32) + pseudo
        moved[...] = momentum.astype(bf16)
        nm_out[rows, :] = moved[high]
        share[k, :, core] = (anchor - outer_rate * (pseudo + outer_beta * momentum)).astype(bf16)
        send_share(k).start()

    def ri(k):
        send_share(k).wait_recv()
        rows = pl.ds(pl.multiple_of(k * ROWS, ROWS), ROWS)
        for q in range(4):
            np_out[rows, q * QUARTER : (q + 1) * QUARTER] = share[k, q // 2, q % 2]

    def forward(n):
        cols = pl.ds(pl.multiple_of(n * 256, 256), 256)
        total = jnp.dot(h[...], wf[:, :, :, :, cols].reshape(FF, 256), preferred_element_type=f32)
        lo[:, cols] = (total * (FF ** (-0.5))).astype(bf16)
    def backward(n):
        @pl.loop(0, 4)
        def _(c):
            units = pl.ds(pl.multiple_of(n * 1024 + c * 256, 256), 256)
            back = lax.dot_general(
                g[...], wf[n, c].reshape(256, D), (((1,), (1,)), ((), ())), preferred_element_type=f32
            )
            ig[:, units] = (back * (D ** (-0.5))).astype(bf16)

    def shard_in(r):
        copy(w_hbm, wf.at[y, x, z], wz_ss.at[3 - r], wz_rs.at[3 - r], zpair).wait_recv()

    for r in (1, 3, 2):
        wz(r).start()
    send_g().start()
    load_w.wait()
    ga(0)
    gb(0)
    gc(0)
    load_h.wait()

    @pl.loop(0, 32)
    def _(n):
        d, m = n // 2, lax.rem(n, 2)
        turned = h[:, pl.ds(pl.multiple_of(n * 128, 128), 128)].T
        for par in (0, 1):
            ht[par, :, d, m] = turned[par * BLOCK : (par + 1) * BLOCK].reshape(CHUNKS, ROWS, LOCAL)

    @pl.loop(0, CHUNKS)
    def _(k):
        send_h(k).start()

    send_anchor().start()
    send_momentum().start()
    for load in load_small:
        load.wait()
    load_g.wait()
    shard_in(1)
    ga(1)
    gb(1)

    @pl.loop(1, 4)
    def _(r):
        gc(r)

        @pl.when(r < 3)
        def _():
            shard_in(r + 1)
            ga(r + 1)

        gd(r - 1)

        @pl.when(r < 3)
        def _():
            gb(r + 1)

        own(r - 1)

    send_g().wait_recv()

    last = CHUNKS - 1

    @pl.loop(0, CHUNKS)
    def _(t):
        send_h(t).wait_recv()
        ra(t)

        @pl.when(t >= 1)
        def _():
            rd(t - 1)

        @pl.when(t == 0)
        def _():
            gd(3)
            own(3)

            @pl.loop(0, 4)
            def _(r):
                ge(r)

        forward(t)
        rb(t)
        backward(t)

        @pl.when(t >= 1)
        def _():
            re(t - 1)

        @pl.when(t == last)
        def _():
            @pl.loop(0, last - 1)
            def _(k):
                rf(k)

        rc(t)

    @pl.loop(0, last - 1)
    def _(k):
        rg(k)

    rd(last)
    send_anchor().wait_recv()
    send_momentum().wait_recv()
    rf(last - 1)
    re(last)
    rg(last - 1)

    @pl.loop(0, last - 1)
    def _(k):
        rh(k)

    rf(last)
    rg(last)
    rh(last - 1)

    @pl.loop(0, last)
    def _(k):
        ri(k)

    rh(last)
    ri(last)

    for r in (1, 2, 3):
        wz(r).wait_send()
    send_g().wait_send()
    send_anchor().wait_send()
    send_momentum().wait_send()

    @pl.loop(0, 4)
    def _(k):
        for hf, i in both:
            for kind in range(4):
                gather(kind, k, hf, i).wait_send()
            for kind in range(3):
                reduce1(kind, k, hf, i).wait_send()
                reduce2(kind, k, hf, i).wait_send()
        send_h(k).wait_send()
        send_z(k).wait_send()
        send_inner(k).wait_send()
        send_both(k).wait_send()
        send_share(k).wait_send()


def local(hidden_rows, out_grad, params, first_moment, second_moment, anchor, outer_momentum):
    shapes = [(LOCAL, D), (LOCAL, FF), (BLOCK, D), (BLOCK, D), (BLOCK, D), (BLOCK, QUARTER)]
    anywhere = pl.BlockSpec(memory_space=pl.ANY)
    vmem = pl.BlockSpec(memory_space=pltpu.VMEM)
    dma = pltpu.SemaphoreType.DMA
    n = CHUNKS
    step1 = pltpu.VMEM((n, 2, 2, 2, 2 * ROWS, HALF), f32)
    step2 = pltpu.VMEM((n, 2, 2, ROWS, HALF), f32)

    quarters = pltpu.VMEM((n, 2, ROWS, QUARTER), f32)

    def pair(*shape):
        return [dma(shape), dma(shape)]

    out = pl.pallas_call(
        kernel,
        out_shape=[pltpu.VMEM(shape, bf16) for shape in shapes],
        in_specs=[anywhere] * 7,
        out_specs=[vmem] * 6,
        scratch_shapes=[
            pltpu.VMEM((LOCAL, FF), bf16),
            pltpu.VMEM((LOCAL, D), bf16),
            pltpu.VMEM((BLOCK, D), bf16),
            pltpu.VMEM((BLOCK, D), bf16),
            pltpu.VMEM((LOCAL, D), bf16),
            pltpu.VMEM((4, 4, 4, BLOCK, D), bf16),
            pltpu.VMEM((2, n, 16, 2, ROWS, LOCAL), bf16),
            pltpu.VMEM((n, 16, 2, ROWS, LOCAL), bf16),
            pltpu.VMEM((n, 4, 4, 2 * ROWS, D), f32),
            step1, step1, step1,
            pltpu.VMEM((n, 2, 4, 2 * ROWS, HALF), f32),
            step2, step2, step2,
            pltpu.VMEM((n, 2, ROWS, D), f32),
            pltpu.VMEM((n, ROWS, D), f32),
            pltpu.VMEM((n, 2, 2, ROWS, QUARTER), f32),
            quarters, quarters, quarters,
            pltpu.VMEM((2, BLOCK, QUARTER), bf16),
            pltpu.VMEM((2, BLOCK, QUARTER), bf16),
            pltpu.VMEM((2, ROWS, QUARTER), bf16),
            pltpu.VMEM((n, 2, 2, ROWS, QUARTER), bf16),
            dma((7,)),
            *pair(3),
            *pair(4, 4, 2, 2),
            *pair(n + 1),
            *pair(n, 3, 2, 2),
            *pair(n, 3, 2, 2),
            *pair(n),
            *pair(2),
            *pair(n),
            *pair(n),
            *pair(n),
        ],
        compiler_params=pltpu.CompilerParams(
            collective_id=0, has_side_effects=True, vmem_limit_bytes=50 * MIB
        ),
        cost_estimate=pl.CostEstimate(flops=13 * 10**9, bytes_accessed=13 * MIB, transcendentals=0),
        name="step",
    )(hidden_rows[0], out_grad[0], params[0], first_moment[0], second_moment[0], anchor, outer_momentum)
    return (out[0][None], out[1][None], out[2], out[3][None], out[4][None], out[5])


def solution(mesh):
    rows = P("group", "fsdp", None)
    return jax.shard_map(
        local,
        mesh=mesh,
        in_specs=(rows, rows, rows, rows, rows, P("fsdp", "group"), P("fsdp", "group")),
        out_specs=(rows, rows, P("fsdp", None), rows, rows, P("fsdp", "group")),
        check_vma=False,
    )
```

```python
import jax
import jax.numpy as jnp
from jax import lax
from jax.experimental import pallas as pl
from jax.experimental.pallas import tpu as pltpu
from jax.sharding import PartitionSpec as P

D = 1024
FF = 4096
TOKENS = 32768
BLOCK = 64
LOCAL = 512
CHUNKS = 4
ROWS = BLOCK // CHUNKS
LAST = CHUNKS - 1
HALF = D // 2
QUARTER = D // 4
MIB = 1 << 20

beta_first = 0.9
beta_second = 0.95
adam_eps = 1e-08
learn_rate = 0.1
decay_rate = 0.1
outer_rate = 0.7
outer_beta = 0.9

bf16 = jnp.bfloat16
f32 = jnp.float32


def kernel(
    h_hbm, g_hbm, w_hbm, fm_hbm, sm_hbm, an_hbm, om_hbm,
    lo, ig, blocks, nm_out,
    h, g, fm, sm, gr, wf, ht, htr, part, o1, n1, s1, sums, o2, n2, s2, d2, plane, zin,
    inner, inner_in, both_sum, both_in, anchors, momenta, moved, share,
    in_sem,
    wz_ss, wz_rs, ag_ss, ag_rs, ex_ss, ex_rs, r1_ss, r1_rs, r2_ss, r2_rs, d2_ss, d2_rs, zz_ss, zz_rs,
    am_ss, am_rs, gi_ss, gi_rs, gh_ss, gh_rs, np_ss, np_rs,
):
    me = lax.axis_index("fsdp")
    grp = lax.axis_index("group")
    z, x, y = lax.rem(me, 4), lax.rem(me // 4, 4), me // 16
    parity, level = lax.rem(z, 2), z // 2

    def at(xx, yy, zz):
        return {"fsdp": (yy * 4 + xx) * 4 + zz}

    def near(axis, step):
        if axis == 0:
            return at(lax.rem(x + step + 4, 4), y, z)
        return at(x, lax.rem(y + step + 4, 4), z)

    core, high = lax.rem(grp, 2), grp // 2
    other_core = {"group": high * 2 + 1 - core}
    other_half = {"group": (1 - high) * 2 + core}

    def copy(src, dst, ss, rs, device):
        return pltpu.make_async_remote_copy(
            src_ref=src, dst_ref=dst, send_sem=ss, recv_sem=rs, device_id=device, device_id_type=pl.DeviceIdType.MESH
        )

    zpair = at(x, y, z + 1 - 2 * parity)
    zcross = at(x, y, lax.rem(z + 2, 4))
    steps = (1, -1)

    load_g = pltpu.make_async_copy(g_hbm, g, in_sem.at[0])
    load_h = pltpu.make_async_copy(h_hbm, h, in_sem.at[1])
    load_w = pltpu.make_async_copy(w_hbm, wf.at[y, x, z], in_sem.at[2])
    load_w.start()
    load_h.start()
    load_g.start()
    load_small = [
        pltpu.make_async_copy(src, dst, in_sem.at[3 + j])
        for j, (src, dst) in enumerate(
            ((fm_hbm, fm), (sm_hbm, sm), (an_hbm, anchors.at[high]), (om_hbm, momenta.at[high]))
        )
    ]
    for load in load_small:
        load.start()

    barrier = pltpu.get_barrier_semaphore()
    others = [near(a, s) for a in (0, 1) for s in (1, -1, 2)]
    others += [at(x, y, lax.rem(z + r, 4)) for r in (1, 2, 3)]
    others += [other_core, other_half]
    for other in others:
        pl.semaphore_signal(barrier, inc=1, device_id=other, device_id_type=pl.DeviceIdType.MESH)
    pl.semaphore_wait(barrier, len(others))

    def wz(r):
        return copy(w_hbm, wf.at[y, x, z], wz_ss.at[r - 1], wz_rs.at[r - 1], at(x, y, lax.rem(z + r, 4)))

    def gather(kind, r, hf, i):
        step = steps[i]
        zs = lax.rem(z + r, 4)
        cols = pl.ds(hf * HALF, HALF)
        first, second = hf, 1 - hf
        mine, across = (x, y) if hf == 0 else (y, x)
        prev = lax.rem(mine - step + 4, 4)
        back = lax.rem(across - step + 4, 4)
        if kind == 0:
            ref, axis = wf.at[y, x, zs, :, cols], first
        elif kind == 1:
            rows = pl.ds(i * (BLOCK // 2), BLOCK // 2)
            ref = wf.at[y, prev, zs, rows, cols] if hf == 0 else wf.at[prev, x, zs, rows, cols]
            axis = first
        elif kind == 2:
            ref = wf.at[y, :, zs, :, cols] if hf == 0 else wf.at[:, x, zs, :, cols]
            axis = second
        else:
            pair = pl.ds(2 * i, 2)
            ref = wf.at[back, pair, zs, :, cols] if hf == 0 else wf.at[pair, back, zs, :, cols]
            axis = second
        return copy(ref, ref, ag_ss.at[r, kind, hf, i], ag_rs.at[r, kind, hf, i], near(axis, step))

    def send_g():
        return copy(g_hbm, gr, ex_ss.at[CHUNKS], ex_rs.at[CHUNKS], zpair)

    def send_h(k):
        return copy(ht.at[1 - parity, k], htr.at[k], ex_ss.at[k], ex_rs.at[k], zpair)

    def chunk1(k, hf, dest, side):
        cols = pl.ds(hf * HALF, HALF)
        two = pl.ds(2 * side, 2)
        return part.at[k, two, dest, :, cols] if hf == 0 else part.at[k, dest, two, :, cols]

    def reduce1(kind, k, hf, i):
        step = steps[i]
        mine = x if hf == 0 else y
        if kind == 0:
            src, dst = chunk1(k, hf, lax.rem(mine + 2, 4), i), o1.at[k, hf, i]
        elif kind == 1:
            src, dst = chunk1(k, hf, lax.rem(mine + step + 4, 4), 1 - i), n1.at[k, hf, i]
        else:
            src, dst = o1.at[k, hf, i], s1.at[k, hf, i]
        return copy(src, dst, r1_ss.at[k, kind, hf, i], r1_rs.at[k, kind, hf, i], near(hf, step))

    def chunk2(k, hf, dest, side):
        return sums.at[k, hf, dest, pl.ds(side * ROWS, ROWS)]

    def reduce2(kind, k, hf, i):
        step = steps[i]
        mine = y if hf == 0 else x
        if kind == 0:
            src, dst = chunk2(k, hf, lax.rem(mine + 2, 4), i), o2.at[k, hf, i]
        elif kind == 1:
            src, dst = chunk2(k, hf, lax.rem(mine + step + 4, 4), 1 - i), n2.at[k, hf, i]
        else:
            src, dst = o2.at[k, hf, i], s2.at[k, hf, i]
        return copy(src, dst, r2_ss.at[k, kind, hf, i], r2_rs.at[k, kind, hf, i], near(1 - hf, step))

    def direct2(hf, j):
        mine = y if hf == 0 else x
        dest = lax.rem(mine + j + 1, 4)
        return copy(sums.at[LAST, hf, dest], d2.at[hf, j], d2_ss.at[hf, j], d2_rs.at[hf, j], near(1 - hf, j + 1))

    def send_z(k):
        return copy(plane.at[k, 1 - level], zin.at[k], zz_ss.at[k], zz_rs.at[k], zcross)

    def send_anchor():
        return copy(an_hbm, anchors.at[high], am_ss.at[0], am_rs.at[0], other_half)

    def send_momentum():
        return copy(om_hbm, momenta.at[high], am_ss.at[1], am_rs.at[1], other_half)

    def send_inner(k):
        return copy(inner.at[k, :, 1 - core], inner_in.at[k], gi_ss.at[k], gi_rs.at[k], other_core)

    def send_both(k):
        return copy(both_sum.at[k], both_in.at[k], gh_ss.at[k], gh_rs.at[k], other_half)

    def send_share(k):
        ref = share.at[k, :, core]
        return copy(ref, ref, np_ss.at[k], np_rs.at[k], other_core)

    both = [(hf, i) for hf in (0, 1) for i in (0, 1)]

    def ga(r):
        for hf, i in both:
            gather(0, r, hf, i).start()

    def gb(r):
        for hf, i in both:
            gather(0, r, hf, i).wait_recv()
            gather(1, r, hf, i).start()

    def gc(r):
        for hf, i in both:
            gather(1, r, hf, i).wait_recv()
        for hf, i in both:
            gather(2, r, hf, i).start()

    def gd(r):
        for hf, i in both:
            gather(2, r, hf, i).wait_recv()
            gather(3, r, hf, i).start()

    def ge(r):
        for hf, i in both:
            gather(3, r, hf, i).wait_recv()

    def own(k):
        @pl.loop(0, D // 256)
        def _(n):
            cols = pl.ds(pl.multiple_of(n * 256, 256), 256)
            mine = ht[parity, k].reshape(32 * ROWS, LOCAL)
            total = jnp.dot(mine, g[:, cols], preferred_element_type=f32)
            part[k, :, :, :, cols] = total.reshape(4, 4, 2 * ROWS, 256)

    def ra(k):
        @pl.loop(0, 2)
        def _(hf):
            @pl.loop(0, 2)
            def _(n):
                cols = pl.ds(pl.multiple_of(hf * HALF + n * 256, 256), 256)
                theirs = htr[k].reshape(32 * ROWS, LOCAL)
                total = jnp.dot(theirs, gr[:, cols], preferred_element_type=f32)
                part[k, :, :, :, cols] += total.reshape(4, 4, 2 * ROWS, 256)

            for half in (0, 1):

                @pl.when(hf == half)
                def _():
                    for kind in (0, 1):
                        for i in (0, 1):
                            reduce1(kind, k, half, i).start()

    def rb(k):
        for hf, i in both:
            mine = x if hf == 0 else y
            reduce1(0, k, hf, i).wait_recv()
            o1[k, hf, i] = o1[k, hf, i] + chunk1(k, hf, lax.rem(mine + steps[i] + 4, 4), i)[...]
            reduce1(2, k, hf, i).start()

    def sum1(k, hf):
        mine = x if hf == 0 else y
        for i in (0, 1):
            reduce1(1, k, hf, 1 - i).wait_recv()
            reduce1(2, k, hf, i).wait_recv()
            sums[k, hf, pl.ds(2 * i, 2)] = (chunk1(k, hf, mine, i)[...] + s1[k, hf, i]) + n1[k, hf, 1 - i]

    def rc(k):
        for hf in (0, 1):
            sum1(k, hf)
            for kind in (0, 1):
                for i in (0, 1):
                    reduce2(kind, k, hf, i).start()

    def rc_last():
        for hf in (0, 1):
            sum1(LAST, hf)
            for j in (1, 0, 2):
                direct2(hf, j).start()

    def re_last():
        for hf in (0, 1):
            mine = y if hf == 0 else x
            for j in (0, 2, 1):
                direct2(hf, j).wait_recv()
            total = (sums[LAST, hf, mine] + d2[hf, 0]) + (d2[hf, 1] + d2[hf, 2])
            plane[LAST, :, :, pl.ds(hf * HALF, HALF)] = total.reshape(2, ROWS, HALF)
        send_z(LAST).start()

    def rd(k):
        for hf, i in both:
            mine = y if hf == 0 else x
            reduce2(0, k, hf, i).wait_recv()
            o2[k, hf, i] = o2[k, hf, i] + chunk2(k, hf, lax.rem(mine + steps[i] + 4, 4), i)[...]
            reduce2(2, k, hf, i).start()

    def re(k):
        for hf in (0, 1):
            mine = y if hf == 0 else x
            for i in (0, 1):
                reduce2(1, k, hf, 1 - i).wait_recv()
                reduce2(2, k, hf, i).wait_recv()
                plane[k, i, :, pl.ds(hf * HALF, HALF)] = (chunk2(k, hf, mine, i)[...] + s2[k, hf, i]) + n2[k, hf, 1 - i]
        send_z(k).start()

    def rf(k):
        send_z(k).wait_recv()
        rows = pl.ds(pl.multiple_of(k * ROWS, ROWS), ROWS)
        grad = (plane[k, level] + zin[k]) * (TOKENS ** (-0.5))
        first = beta_first * fm[rows, :].astype(f32) + (1.0 - beta_first) * grad
        second = beta_second * sm[rows, :].astype(f32) + (1.0 - beta_second) * grad * grad
        weight = wf[y, x, z, rows, :].astype(f32)
        blocks[1, rows, :] = first.astype(bf16)
        blocks[2, rows, :] = second.astype(bf16)
        fresh = weight - learn_rate * (first / (jnp.sqrt(second) + adam_eps) + decay_rate * weight)
        for q in range(4):
            inner[k, q // 2, q % 2] = fresh[:, q * QUARTER : (q + 1) * QUARTER]
        send_inner(k).start()

    def rg(k):
        send_inner(k).wait_recv()
        both_sum[k] = inner[k, :, core] + inner_in[k]
        send_both(k).start()

    def rh(k):
        send_both(k).wait_recv()
        rows = pl.ds(pl.multiple_of(k * ROWS, ROWS), ROWS)
        anchor = anchors[:, rows].astype(f32)
        pseudo = anchor - (both_sum[k] + both_in[k]) / 4
        momentum = outer_beta * momenta[:, rows].astype(f32) + pseudo
        moved[...] = momentum.astype(bf16)
        nm_out[rows, :] = moved[high]
        share[k, :, core] = (anchor - outer_rate * (pseudo + outer_beta * momentum)).astype(bf16)
        send_share(k).start()

    def ri(k):
        send_share(k).wait_recv()
        rows = pl.ds(pl.multiple_of(k * ROWS, ROWS), ROWS)
        for q in range(4):
            blocks[0, rows, q * QUARTER : (q + 1) * QUARTER] = share[k, q // 2, q % 2]

    def forward(n):
        cols = pl.ds(pl.multiple_of(n * 256, 256), 256)
        total = jnp.dot(h[...], wf[:, :, :, :, cols].reshape(FF, 256), preferred_element_type=f32)
        lo[:, cols] = (total * (FF ** (-0.5))).astype(bf16)
    def backward(n):
        @pl.loop(0, 4)
        def _(c):
            units = pl.ds(pl.multiple_of(n * 1024 + c * 256, 256), 256)
            back = lax.dot_general(
                g[...], wf[n, c].reshape(256, D), (((1,), (1,)), ((), ())), preferred_element_type=f32
            )
            ig[:, units] = (back * (D ** (-0.5))).astype(bf16)

    def sent1(k):
        for hf, i in both:
            for kind in range(3):
                reduce1(kind, k, hf, i).wait_send()
        send_h(k).wait_send()

    def sent2(k):
        for hf, i in both:
            for kind in range(3):
                reduce2(kind, k, hf, i).wait_send()

    def shard_in(r):
        copy(w_hbm, wf.at[y, x, z], wz_ss.at[3 - r], wz_rs.at[3 - r], zpair).wait_recv()

    for r in (3, 2, 1):
        wz(r).start()
    send_g().start()
    load_w.wait()
    ga(0)
    gb(0)
    gc(0)
    load_h.wait()

    @pl.loop(0, 32)
    def _(n):
        d, m = n // 2, lax.rem(n, 2)
        turned = h[:, pl.ds(pl.multiple_of(n * 128, 128), 128)].T
        for par in (0, 1):
            ht[par, :, d, m] = turned[par * BLOCK : (par + 1) * BLOCK].reshape(CHUNKS, ROWS, LOCAL)

    @pl.loop(0, CHUNKS)
    def _(k):
        send_h(k).start()

    send_anchor().start()
    send_momentum().start()
    for load in load_small:
        load.wait()
    load_g.wait()
    shard_in(1)
    ga(1)
    gb(1)

    @pl.loop(1, 4)
    def _(r):
        gc(r)

        @pl.when(r < 3)
        def _():
            shard_in(r + 1)
            ga(r + 1)

        gd(r - 1)

        @pl.when(r < 3)
        def _():
            gb(r + 1)

        own(r - 1)

    send_g().wait_recv()

    @pl.loop(0, CHUNKS)
    def _(t):
        for hf, i in both:
            for kind in range(4):
                gather(kind, t, hf, i).wait_send()

        @pl.when(t >= 1)
        def _():
            sent1(t - 1)

        @pl.when(t >= 2)
        def _():
            sent2(t - 2)

        send_h(t).wait_recv()
        ra(t)

        @pl.when(t == 0)
        def _():
            gd(3)
            own(3)

            @pl.loop(0, 4)
            def _(r):
                ge(r)

        @pl.when(t >= 2)
        def _():
            re(t - 2)

        forward(t)

        @pl.when(t >= 1)
        def _():
            rc(t - 1)

        rb(t)

        @pl.when(t >= 1)
        def _():
            rd(t - 1)

        backward(t)

    re(LAST - 1)

    @pl.loop(0, LAST - 1)
    def _(k):
        rf(k)

    rc_last()
    rf(LAST - 1)

    @pl.loop(0, LAST - 1)
    def _(k):
        rg(k)

    send_anchor().wait_recv()
    send_momentum().wait_recv()
    re_last()
    rg(LAST - 1)

    @pl.loop(0, LAST - 1)
    def _(k):
        rh(k)

    rf(LAST)
    rg(LAST)
    rh(LAST - 1)

    @pl.loop(0, LAST)
    def _(k):
        ri(k)

    for r in (1, 2, 3):
        wz(r).wait_send()
    send_g().wait_send()
    send_anchor().wait_send()
    send_momentum().wait_send()
    sent1(LAST)
    sent2(LAST - 1)
    for hf in (0, 1):
        for j in range(3):
            direct2(hf, j).wait_send()

    @pl.loop(0, CHUNKS)
    def _(k):
        send_z(k).wait_send()
        send_inner(k).wait_send()

    @pl.loop(0, LAST)
    def _(k):
        send_both(k).wait_send()
        send_share(k).wait_send()

    rh(LAST)
    ri(LAST)
    send_both(LAST).wait_send()
    send_share(LAST).wait_send()


def local(hidden_rows, out_grad, params, first_moment, second_moment, anchor, outer_momentum):
    shapes = [(LOCAL, D), (LOCAL, FF), (3, BLOCK, D), (BLOCK, QUARTER)]
    anywhere = pl.BlockSpec(memory_space=pl.ANY)
    vmem = pl.BlockSpec(memory_space=pltpu.VMEM)
    dma = pltpu.SemaphoreType.DMA
    n = CHUNKS
    step1 = pltpu.VMEM((n, 2, 2, 2, 2 * ROWS, HALF), f32)
    step2 = pltpu.VMEM((n, 2, 2, ROWS, HALF), f32)

    quarters = pltpu.VMEM((n, 2, ROWS, QUARTER), f32)

    def pair(*shape):
        return [dma(shape), dma(shape)]

    out = pl.pallas_call(
        kernel,
        out_shape=[pltpu.VMEM(shape, bf16) for shape in shapes],
        in_specs=[anywhere] * 7,
        out_specs=[vmem] * 4,
        scratch_shapes=[
            pltpu.VMEM((LOCAL, FF), bf16),
            pltpu.VMEM((LOCAL, D), bf16),
            pltpu.VMEM((BLOCK, D), bf16),
            pltpu.VMEM((BLOCK, D), bf16),
            pltpu.VMEM((LOCAL, D), bf16),
            pltpu.VMEM((4, 4, 4, BLOCK, D), bf16),
            pltpu.VMEM((2, n, 16, 2, ROWS, LOCAL), bf16),
            pltpu.VMEM((n, 16, 2, ROWS, LOCAL), bf16),
            pltpu.VMEM((n, 4, 4, 2 * ROWS, D), f32),
            step1, step1, step1,
            pltpu.VMEM((n, 2, 4, 2 * ROWS, HALF), f32),
            step2, step2, step2,
            pltpu.VMEM((2, 3, 2 * ROWS, HALF), f32),
            pltpu.VMEM((n, 2, ROWS, D), f32),
            pltpu.VMEM((n, ROWS, D), f32),
            pltpu.VMEM((n, 2, 2, ROWS, QUARTER), f32),
            quarters, quarters, quarters,
            pltpu.VMEM((2, BLOCK, QUARTER), bf16),
            pltpu.VMEM((2, BLOCK, QUARTER), bf16),
            pltpu.VMEM((2, ROWS, QUARTER), bf16),
            pltpu.VMEM((n, 2, 2, ROWS, QUARTER), bf16),
            dma((7,)),
            *pair(3),
            *pair(4, 4, 2, 2),
            *pair(n + 1),
            *pair(n, 3, 2, 2),
            *pair(n, 3, 2, 2),
            *pair(2, 3),
            *pair(n),
            *pair(2),
            *pair(n),
            *pair(n),
            *pair(n),
        ],
        compiler_params=pltpu.CompilerParams(
            collective_id=0, has_side_effects=True, vmem_limit_bytes=50 * MIB
        ),
        cost_estimate=pl.CostEstimate(flops=13 * 10**9, bytes_accessed=13 * MIB, transcendentals=0),
        name="step",
    )(hidden_rows[0], out_grad[0], params[0], first_moment[0], second_moment[0], anchor, outer_momentum)
    return (out[0][None], out[1][None], out[2][0], out[2][1:2], out[2][2:3], out[3])


def solution(mesh):
    rows = P("group", "fsdp", None)
    return jax.shard_map(
        local,
        mesh=mesh,
        in_specs=(rows, rows, rows, rows, rows, P("fsdp", "group"), P("fsdp", "group")),
        out_specs=(rows, rows, P("fsdp", None), rows, rows, P("fsdp", "group")),
        check_vma=False,
    )
```

```python
import jax
import jax.numpy as jnp
from jax import lax
from jax.experimental import pallas as pl
from jax.experimental.pallas import tpu as pltpu
from jax.sharding import PartitionSpec as P

D = 1024
FF = 4096
TOKENS = 32768
BLOCK = 64
LOCAL = 512
CHUNKS = 4
ROWS = BLOCK // CHUNKS
LAST = CHUNKS - 1
HALF = D // 2
QUARTER = D // 4
MIB = 1 << 20

beta_first = 0.9
beta_second = 0.95
adam_eps = 1e-08
learn_rate = 0.1
decay_rate = 0.1
outer_rate = 0.7
outer_beta = 0.9

bf16 = jnp.bfloat16
f32 = jnp.float32


def kernel(
    h_hbm, g_hbm, w_hbm, fm_hbm, sm_hbm, an_hbm, om_hbm,
    lo, ig, blocks, nm_out,
    h, g, fm, sm, gr, wf, ht, htr, part, o1, n1, s1, sums, o2, n2, s2, d2, plane, zin,
    inner, inner_in, both_sum, both_in, anchors, momenta, moved, share,
    in_sem,
    wz_ss, wz_rs, ag_ss, ag_rs, ex_ss, ex_rs, r1_ss, r1_rs, r2_ss, r2_rs, d2_ss, d2_rs, zz_ss, zz_rs,
    am_ss, am_rs, gi_ss, gi_rs, gh_ss, gh_rs, np_ss, np_rs,
):
    me = lax.axis_index("fsdp")
    grp = lax.axis_index("group")
    z, x, y = lax.rem(me, 4), lax.rem(me // 4, 4), me // 16
    parity, level = lax.rem(z, 2), z // 2

    def at(xx, yy, zz):
        return {"fsdp": (yy * 4 + xx) * 4 + zz}

    def near(axis, step):
        if axis == 0:
            return at(lax.rem(x + step + 4, 4), y, z)
        return at(x, lax.rem(y + step + 4, 4), z)

    core, high = lax.rem(grp, 2), grp // 2
    other_core = {"group": high * 2 + 1 - core}
    other_half = {"group": (1 - high) * 2 + core}

    def copy(src, dst, ss, rs, device):
        return pltpu.make_async_remote_copy(
            src_ref=src, dst_ref=dst, send_sem=ss, recv_sem=rs, device_id=device, device_id_type=pl.DeviceIdType.MESH
        )

    zpair = at(x, y, z + 1 - 2 * parity)
    zcross = at(x, y, lax.rem(z + 2, 4))
    steps = (1, -1)

    load_g = pltpu.make_async_copy(g_hbm, g, in_sem.at[0])
    load_h = pltpu.make_async_copy(h_hbm, h, in_sem.at[1])
    load_w = pltpu.make_async_copy(w_hbm, wf.at[y, x, z], in_sem.at[2])
    load_w.start()
    load_h.start()
    load_g.start()
    load_small = [
        pltpu.make_async_copy(src, dst, in_sem.at[3 + j])
        for j, (src, dst) in enumerate(
            ((fm_hbm, fm), (sm_hbm, sm), (an_hbm, anchors.at[high]), (om_hbm, momenta.at[high]))
        )
    ]
    for load in load_small:
        load.start()

    barrier = pltpu.get_barrier_semaphore()
    others = [near(a, s) for a in (0, 1) for s in (1, -1, 2)]
    others += [at(x, y, lax.rem(z + r, 4)) for r in (1, 2, 3)]
    others += [other_core, other_half]
    for other in others:
        pl.semaphore_signal(barrier, inc=1, device_id=other, device_id_type=pl.DeviceIdType.MESH)
    pl.semaphore_wait(barrier, len(others))

    def wz(r):
        return copy(w_hbm, wf.at[y, x, z], wz_ss.at[r - 1], wz_rs.at[r - 1], at(x, y, lax.rem(z + r, 4)))

    def gather(kind, r, hf, i):
        step = steps[i]
        zs = lax.rem(z + r, 4)
        cols = pl.ds(hf * HALF, HALF)
        first, second = hf, 1 - hf
        mine, across = (x, y) if hf == 0 else (y, x)
        prev = lax.rem(mine - step + 4, 4)
        back = lax.rem(across - step + 4, 4)
        if kind == 0:
            ref, axis = wf.at[y, x, zs, :, cols], first
        elif kind == 1:
            rows = pl.ds(i * (BLOCK // 2), BLOCK // 2)
            ref = wf.at[y, prev, zs, rows, cols] if hf == 0 else wf.at[prev, x, zs, rows, cols]
            axis = first
        elif kind == 2:
            ref = wf.at[y, :, zs, :, cols] if hf == 0 else wf.at[:, x, zs, :, cols]
            axis = second
        else:
            pair = pl.ds(2 * i, 2)
            ref = wf.at[back, pair, zs, :, cols] if hf == 0 else wf.at[pair, back, zs, :, cols]
            axis = second
        return copy(ref, ref, ag_ss.at[r, kind, hf, i], ag_rs.at[r, kind, hf, i], near(axis, step))

    def send_g():
        return copy(g_hbm, gr, ex_ss.at[CHUNKS], ex_rs.at[CHUNKS], zpair)

    def send_h(k):
        return copy(ht.at[1 - parity, k], htr.at[k], ex_ss.at[k], ex_rs.at[k], zpair)

    def chunk1(k, hf, dest, side):
        cols = pl.ds(hf * HALF, HALF)
        two = pl.ds(2 * side, 2)
        return part.at[k, two, dest, :, cols] if hf == 0 else part.at[k, dest, two, :, cols]

    def reduce1(kind, k, hf, i):
        step = steps[i]
        mine = x if hf == 0 else y
        if kind == 0:
            src, dst = chunk1(k, hf, lax.rem(mine + 2, 4), i), o1.at[k, hf, i]
        elif kind == 1:
            src, dst = chunk1(k, hf, lax.rem(mine + step + 4, 4), 1 - i), n1.at[k, hf, i]
        else:
            src, dst = o1.at[k, hf, i], s1.at[k, hf, i]
        return copy(src, dst, r1_ss.at[k, kind, hf, i], r1_rs.at[k, kind, hf, i], near(hf, step))

    def chunk2(k, hf, dest, side):
        return sums.at[k, hf, dest, pl.ds(side * ROWS, ROWS)]

    def reduce2(kind, k, hf, i):
        step = steps[i]
        mine = y if hf == 0 else x
        if kind == 0:
            src, dst = chunk2(k, hf, lax.rem(mine + 2, 4), i), o2.at[k, hf, i]
        elif kind == 1:
            src, dst = chunk2(k, hf, lax.rem(mine + step + 4, 4), 1 - i), n2.at[k, hf, i]
        else:
            src, dst = o2.at[k, hf, i], s2.at[k, hf, i]
        return copy(src, dst, r2_ss.at[k, kind, hf, i], r2_rs.at[k, kind, hf, i], near(1 - hf, step))

    def direct2(hf, j):
        mine = y if hf == 0 else x
        dest = lax.rem(mine + j + 1, 4)
        return copy(sums.at[LAST, hf, dest], d2.at[hf, j], d2_ss.at[hf, j], d2_rs.at[hf, j], near(1 - hf, j + 1))

    def send_z(k):
        return copy(plane.at[k, 1 - level], zin.at[k], zz_ss.at[k], zz_rs.at[k], zcross)

    def send_anchor():
        return copy(an_hbm, anchors.at[high], am_ss.at[0], am_rs.at[0], other_half)

    def send_momentum():
        return copy(om_hbm, momenta.at[high], am_ss.at[1], am_rs.at[1], other_half)

    def send_z_half(hf):
        cols = pl.ds(hf * HALF, HALF)
        src, dst = plane.at[LAST, 1 - level, :, cols], zin.at[LAST, :, cols]
        return copy(src, dst, zz_ss.at[LAST + hf], zz_rs.at[LAST + hf], zcross)

    def send_inner(k):
        return copy(inner.at[k, :, 1 - core], inner_in.at[k], gi_ss.at[k], gi_rs.at[k], other_core)

    def send_both(k):
        return copy(both_sum.at[k], both_in.at[k], gh_ss.at[k], gh_rs.at[k], other_half)

    def send_share(k):
        ref = share.at[k, :, core]
        return copy(ref, ref, np_ss.at[k], np_rs.at[k], other_core)

    both = [(hf, i) for hf in (0, 1) for i in (0, 1)]

    def ga(r):
        for hf, i in both:
            gather(0, r, hf, i).start()

    def gb(r):
        for hf, i in both:
            gather(0, r, hf, i).wait_recv()
            gather(1, r, hf, i).start()

    def gc(r):
        for hf, i in both:
            gather(1, r, hf, i).wait_recv()
        for hf, i in both:
            gather(2, r, hf, i).start()

    def gd(r):
        for hf, i in both:
            gather(2, r, hf, i).wait_recv()
            gather(3, r, hf, i).start()

    def ge(r):
        for hf, i in both:
            gather(3, r, hf, i).wait_recv()

    def own(k):
        @pl.loop(0, D // 256)
        def _(n):
            cols = pl.ds(pl.multiple_of(n * 256, 256), 256)
            mine = ht[parity, k].reshape(32 * ROWS, LOCAL)
            total = jnp.dot(mine, g[:, cols], preferred_element_type=f32)
            part[k, :, :, :, cols] = total.reshape(4, 4, 2 * ROWS, 256)

    def ra(k):
        @pl.loop(0, 2)
        def _(hf):
            @pl.loop(0, 2)
            def _(n):
                cols = pl.ds(pl.multiple_of(hf * HALF + n * 256, 256), 256)
                theirs = htr[k].reshape(32 * ROWS, LOCAL)
                total = jnp.dot(theirs, gr[:, cols], preferred_element_type=f32)
                part[k, :, :, :, cols] += total.reshape(4, 4, 2 * ROWS, 256)

            for half in (0, 1):

                @pl.when(hf == half)
                def _():
                    for kind in (0, 1):
                        for i in (0, 1):
                            reduce1(kind, k, half, i).start()

    def rb(k):
        for hf, i in both:
            mine = x if hf == 0 else y
            reduce1(0, k, hf, i).wait_recv()
            o1[k, hf, i] = o1[k, hf, i] + chunk1(k, hf, lax.rem(mine + steps[i] + 4, 4), i)[...]
            reduce1(2, k, hf, i).start()

    def sum1(k, hf):
        mine = x if hf == 0 else y
        for i in (0, 1):
            reduce1(1, k, hf, 1 - i).wait_recv()
            reduce1(2, k, hf, i).wait_recv()
            sums[k, hf, pl.ds(2 * i, 2)] = (chunk1(k, hf, mine, i)[...] + s1[k, hf, i]) + n1[k, hf, 1 - i]

    def rc(k):
        for hf in (0, 1):
            sum1(k, hf)
            for kind in (0, 1):
                for i in (0, 1):
                    reduce2(kind, k, hf, i).start()

    def rc_last():
        for hf in (0, 1):
            sum1(LAST, hf)
            for j in (1, 0, 2):
                direct2(hf, j).start()

    def re_last():
        for hf in (0, 1):
            mine = y if hf == 0 else x
            for j in (0, 2, 1):
                direct2(hf, j).wait_recv()
            total = (sums[LAST, hf, mine] + d2[hf, 0]) + (d2[hf, 1] + d2[hf, 2])
            cols = pl.ds(hf * HALF, HALF)
            plane[LAST, :, :, cols] = total.reshape(2, ROWS, HALF)
            send_z_half(hf).start()

    def rd(k):
        for hf, i in both:
            mine = y if hf == 0 else x
            reduce2(0, k, hf, i).wait_recv()
            o2[k, hf, i] = o2[k, hf, i] + chunk2(k, hf, lax.rem(mine + steps[i] + 4, 4), i)[...]
            reduce2(2, k, hf, i).start()

    def re(k):
        for hf in (0, 1):
            mine = y if hf == 0 else x
            for i in (0, 1):
                reduce2(1, k, hf, 1 - i).wait_recv()
                reduce2(2, k, hf, i).wait_recv()
                plane[k, i, :, pl.ds(hf * HALF, HALF)] = (chunk2(k, hf, mine, i)[...] + s2[k, hf, i]) + n2[k, hf, 1 - i]
        send_z(k).start()

    def rf(k):
        if isinstance(k, int) and k == LAST:
            for hf in (0, 1):
                send_z_half(hf).wait_recv()
        else:
            send_z(k).wait_recv()
        rows = pl.ds(pl.multiple_of(k * ROWS, ROWS), ROWS)
        grad = (plane[k, level] + zin[k]) * (TOKENS ** (-0.5))
        first = beta_first * fm[rows, :].astype(f32) + (1.0 - beta_first) * grad
        second = beta_second * sm[rows, :].astype(f32) + (1.0 - beta_second) * grad * grad
        weight = wf[y, x, z, rows, :].astype(f32)
        blocks[1, rows, :] = first.astype(bf16)
        blocks[2, rows, :] = second.astype(bf16)
        fresh = weight - learn_rate * (first / (jnp.sqrt(second) + adam_eps) + decay_rate * weight)
        for q in range(4):
            inner[k, q // 2, q % 2] = fresh[:, q * QUARTER : (q + 1) * QUARTER]
        send_inner(k).start()

    def rg(k):
        send_inner(k).wait_recv()
        both_sum[k] = inner[k, :, core] + inner_in[k]
        send_both(k).start()

    def rh(k):
        send_both(k).wait_recv()
        rows = pl.ds(pl.multiple_of(k * ROWS, ROWS), ROWS)
        anchor = anchors[:, rows].astype(f32)
        pseudo = anchor - (both_sum[k] + both_in[k]) / 4
        momentum = outer_beta * momenta[:, rows].astype(f32) + pseudo
        moved[...] = momentum.astype(bf16)
        nm_out[rows, :] = moved[high]
        share[k, :, core] = (anchor - outer_rate * (pseudo + outer_beta * momentum)).astype(bf16)
        send_share(k).start()

    def ri(k):
        send_share(k).wait_recv()
        rows = pl.ds(pl.multiple_of(k * ROWS, ROWS), ROWS)
        for q in range(4):
            blocks[0, rows, q * QUARTER : (q + 1) * QUARTER] = share[k, q // 2, q % 2]

    def forward(n):
        cols = pl.ds(pl.multiple_of(n * 256, 256), 256)
        total = jnp.dot(h[...], wf[:, :, :, :, cols].reshape(FF, 256), preferred_element_type=f32)
        lo[:, cols] = (total * (FF ** (-0.5))).astype(bf16)
    def backward(n):
        @pl.loop(0, 4)
        def _(c):
            units = pl.ds(pl.multiple_of(n * 1024 + c * 256, 256), 256)
            back = lax.dot_general(
                g[...], wf[n, c].reshape(256, D), (((1,), (1,)), ((), ())), preferred_element_type=f32
            )
            ig[:, units] = (back * (D ** (-0.5))).astype(bf16)

    def sent1(k):
        for hf, i in both:
            for kind in range(3):
                reduce1(kind, k, hf, i).wait_send()
        send_h(k).wait_send()

    def sent2(k):
        for hf, i in both:
            for kind in range(3):
                reduce2(kind, k, hf, i).wait_send()

    def shard_in(r):
        copy(w_hbm, wf.at[y, x, z], wz_ss.at[3 - r], wz_rs.at[3 - r], zpair).wait_recv()

    for r in (3, 2, 1):
        wz(r).start()
    send_g().start()
    load_w.wait()
    ga(0)
    gb(0)
    gc(0)
    load_h.wait()

    @pl.loop(0, 32)
    def _(n):
        d, m = n // 2, lax.rem(n, 2)
        turned = h[:, pl.ds(pl.multiple_of(n * 128, 128), 128)].T
        for par in (0, 1):
            ht[par, :, d, m] = turned[par * BLOCK : (par + 1) * BLOCK].reshape(CHUNKS, ROWS, LOCAL)

    @pl.loop(0, CHUNKS)
    def _(k):
        send_h(k).start()

    send_anchor().start()
    send_momentum().start()
    for load in load_small:
        load.wait()
    load_g.wait()
    shard_in(1)
    ga(1)
    gb(1)

    @pl.loop(1, 4)
    def _(r):
        gc(r)

        @pl.when(r < 3)
        def _():
            shard_in(r + 1)
            ga(r + 1)

        gd(r - 1)

        @pl.when(r < 3)
        def _():
            gb(r + 1)

        own(r - 1)

    send_g().wait_recv()

    @pl.loop(0, CHUNKS)
    def _(t):
        for hf, i in both:
            for kind in range(4):
                gather(kind, t, hf, i).wait_send()

        @pl.when(t >= 1)
        def _():
            sent1(t - 1)

        @pl.when(t >= 2)
        def _():
            sent2(t - 2)

        send_h(t).wait_recv()
        ra(t)

        @pl.when(t == 0)
        def _():
            gd(3)
            own(3)

            @pl.loop(0, 4)
            def _(r):
                ge(r)

        @pl.when(t >= 2)
        def _():
            re(t - 2)

        @pl.when(t >= 1)
        def _():
            rc(t - 1)

        rb(t)
        forward(t)

        @pl.when(t >= 1)
        def _():
            rd(t - 1)

        backward(t)

    re(LAST - 1)

    @pl.loop(0, LAST - 1)
    def _(k):
        rf(k)

    rc_last()
    rf(LAST - 1)

    @pl.loop(0, LAST - 1)
    def _(k):
        rg(k)

    send_anchor().wait_recv()
    send_momentum().wait_recv()
    re_last()
    rg(LAST - 1)

    @pl.loop(0, LAST - 1)
    def _(k):
        rh(k)

    rf(LAST)
    rg(LAST)
    rh(LAST - 1)

    @pl.loop(0, LAST)
    def _(k):
        ri(k)

    for r in (1, 2, 3):
        wz(r).wait_send()
    send_g().wait_send()
    send_anchor().wait_send()
    send_momentum().wait_send()
    sent1(LAST)
    sent2(LAST - 1)
    for hf in (0, 1):
        for j in range(3):
            direct2(hf, j).wait_send()

    @pl.loop(0, CHUNKS)
    def _(k):
        send_inner(k).wait_send()

    for hf in (0, 1):
        send_z_half(hf).wait_send()

    @pl.loop(0, LAST)
    def _(k):
        send_z(k).wait_send()
        send_both(k).wait_send()
        send_share(k).wait_send()

    rh(LAST)
    ri(LAST)
    send_both(LAST).wait_send()
    send_share(LAST).wait_send()


def local(hidden_rows, out_grad, params, first_moment, second_moment, anchor, outer_momentum):
    shapes = [(LOCAL, D), (LOCAL, FF), (3, BLOCK, D), (BLOCK, QUARTER)]
    anywhere = pl.BlockSpec(memory_space=pl.ANY)
    vmem = pl.BlockSpec(memory_space=pltpu.VMEM)
    dma = pltpu.SemaphoreType.DMA
    n = CHUNKS
    step1 = pltpu.VMEM((n, 2, 2, 2, 2 * ROWS, HALF), f32)
    step2 = pltpu.VMEM((n, 2, 2, ROWS, HALF), f32)

    quarters = pltpu.VMEM((n, 2, ROWS, QUARTER), f32)

    def pair(*shape):
        return [dma(shape), dma(shape)]

    out = pl.pallas_call(
        kernel,
        out_shape=[pltpu.VMEM(shape, bf16) for shape in shapes],
        in_specs=[anywhere] * 7,
        out_specs=[vmem] * 4,
        scratch_shapes=[
            pltpu.VMEM((LOCAL, FF), bf16),
            pltpu.VMEM((LOCAL, D), bf16),
            pltpu.VMEM((BLOCK, D), bf16),
            pltpu.VMEM((BLOCK, D), bf16),
            pltpu.VMEM((LOCAL, D), bf16),
            pltpu.VMEM((4, 4, 4, BLOCK, D), bf16),
            pltpu.VMEM((2, n, 16, 2, ROWS, LOCAL), bf16),
            pltpu.VMEM((n, 16, 2, ROWS, LOCAL), bf16),
            pltpu.VMEM((n, 4, 4, 2 * ROWS, D), f32),
            step1, step1, step1,
            pltpu.VMEM((n, 2, 4, 2 * ROWS, HALF), f32),
            step2, step2, step2,
            pltpu.VMEM((2, 3, 2 * ROWS, HALF), f32),
            pltpu.VMEM((n, 2, ROWS, D), f32),
            pltpu.VMEM((n, ROWS, D), f32),
            pltpu.VMEM((n, 2, 2, ROWS, QUARTER), f32),
            quarters, quarters, quarters,
            pltpu.VMEM((2, BLOCK, QUARTER), bf16),
            pltpu.VMEM((2, BLOCK, QUARTER), bf16),
            pltpu.VMEM((2, ROWS, QUARTER), bf16),
            pltpu.VMEM((n, 2, 2, ROWS, QUARTER), bf16),
            dma((7,)),
            *pair(3),
            *pair(4, 4, 2, 2),
            *pair(n + 1),
            *pair(n, 3, 2, 2),
            *pair(n, 3, 2, 2),
            *pair(2, 3),
            *pair(n + 1),
            *pair(2),
            *pair(n),
            *pair(n),
            *pair(n),
        ],
        compiler_params=pltpu.CompilerParams(
            collective_id=0, has_side_effects=True, vmem_limit_bytes=50 * MIB
        ),
        cost_estimate=pl.CostEstimate(flops=13 * 10**9, bytes_accessed=13 * MIB, transcendentals=0),
        name="step",
    )(hidden_rows[0], out_grad[0], params[0], first_moment[0], second_moment[0], anchor, outer_momentum)
    return (out[0][None], out[1][None], out[2][0], out[2][1:2], out[2][2:3], out[3])


def solution(mesh):
    rows = P("group", "fsdp", None)
    return jax.shard_map(
        local,
        mesh=mesh,
        in_specs=(rows, rows, rows, rows, rows, P("fsdp", "group"), P("fsdp", "group")),
        out_specs=(rows, rows, P("fsdp", None), rows, rows, P("fsdp", "group")),
        check_vma=False,
    )
```
